32 devices in a mesh: groups: 2 (over y), seq: 4 (over z), mp: 2 (over x), rep: 2 (over core).
Axes of the slice: x: 2, y: 2, z: 4, core: 2. Of those that a mesh axis runs over, the one named last changes fastest.
Arguments:
- byte_states: bfloat16 [4096, 1024], P(('groups', 'seq', 'mp', 'rep')), parts along dimension 0, may hold values from -6 to 6
- cotangent: bfloat16 [4096, 1024], P(('groups', 'seq', 'mp', 'rep')), parts along dimension 0, may hold values from -6 to 6
- boundaries: int32 [1024], P('groups'), parts along dimension 0, may hold values from 0 to 2047, as said below
- enc_gain: float32 [1024], replicated, may hold values from 0.25 to 1.75
- w_qkv: bfloat16 [1024, 3072], replicated, may hold values from -1 to 1
- w_out: bfloat16 [1024, 1024], replicated, may hold values from -0.1875 to 0.1875
- pad_vector: float32 [3072], replicated, may hold values from -5 to 5
- main_gain: float32 [4096], replicated, may hold values from 0.25 to 1.75
- gate_w: bfloat16 [4096, 6144], P('seq', ('mp', 'rep')), may hold values from -0.09375 to 0.09375
- up_w: bfloat16 [4096, 6144], P('seq', ('mp', 'rep')), may hold values from -0.09375 to 0.09375
- down_t: bfloat16 [4096, 6144], P('seq', ('mp', 'rep')), may hold values from -0.078125 to 0.078125
Outputs:
- main_out: bfloat16 [1024, 4096], P(('groups', 'seq', 'mp', 'rep')), parts along dimension 0
- span_grad: bfloat16 [1024, 1024], P(('groups', 'seq', 'mp', 'rep')), parts along dimension 0
The draws below stay inside these ranges and needn't reach their ends.
There are 2 independent parts, one for each index of `groups`. The reference program is written for one: setup_inputs(seed, part) draws one part's arguments, and reference() takes and returns one part's arrays. A program takes and returns all parts, laid end to end along the dimension named above; an argument that names none is the same for every part. Nothing has to cross between parts.
Inputs may be any that keep to these rules, and one draw needn't show every extreme that they name: `boundaries`: Sorted, strictly increasing, the first is 0. Every aligned block of 128 bytes holds 1 to 63 span starts, and some block holds exactly 63. The bytes of a seq index are the 4 consecutive blocks that its devices hold. The spans of the owner at seq index s (spans s * 128 to (s + 1) * 128 - 1) start only in the bytes of seq indices s - 1, s and s + 1, at most 23 of them in those of s - 1 and at most 23 in those of s + 1; in every draw some owner has exactly 23 starting in those of s - 1, and some owner exactly 23 in those of s + 1.
All inputs are finite; a program needn't handle non-finite values.
Results may differ from the reference program's by a relative error of at most 0.009.
Values may be sent and summed in bfloat16 or wider, within the bound.
No kernel may reach another device: no remote copies, remote signals or barrier semaphores. Data moves between devices by JAX's collectives and lax.ppermute only.
A program may use at most 128 MiB of HBM per device.

```python
import math
import jax
import jax.numpy as jnp
from jax import lax

D = 4096
E = 1024
HEAD = 128
FF = 6144
WINDOW = 128
BYTES_DEV = 128
SPAN_DEV = 32
LANE = 24
HEADS = 8
NDEV = 16
SEQ_LEN = 2048
SPANS = 512
SPAN_OWN = 128


def sign_pattern(width):
    column = jnp.arange(width, dtype=jnp.int32)
    return jnp.where((column * 37 + 11) // 3 % 2 == 0, 1.0, -1.0).astype(jnp.float32)


def draw_byte_states(key, part):
    key = jax.random.fold_in(key, 31)
    key_noise = jax.random.fold_in(key, 0)
    values = jax.random.truncated_normal(key_noise, -6.0, 6.0, (SEQ_LEN, E), jnp.float32)
    return values.astype(jnp.bfloat16)


def draw_w_qkv(key, part):
    key = jax.random.fold_in(key, 23)
    key_base, key_heads = jax.random.split(key)
    scale = 1.0 / math.sqrt(E)
    base = jax.random.truncated_normal(key_base, -4.0, 4.0, (E, 3 * E), jnp.float32) * scale
    head_signs = jnp.where(jax.random.bernoulli(key_heads, 0.5, (E,)), 1.0, -1.0) / math.sqrt(HEAD)
    planted = 2.0 * scale * sign_pattern(E)[:, None] * head_signs[None, :]
    extra = jnp.concatenate([planted, planted, jnp.zeros((E, E), jnp.float32)], axis=1)
    return (base + extra).astype(jnp.bfloat16)


def draw_boundaries(key, part):
    key = jax.random.fold_in(key, 11)
    key_inner, key_edge, key_sign, key_pick, key_order = jax.random.split(key, 5)
    members = SPAN_OWN // SPAN_DEV
    owner_count = SPANS // SPAN_OWN
    quarter = SPAN_DEV // 4
    largest = LANE - 1
    inner = jax.random.randint(key_inner, (NDEV,), -quarter, quarter + 1)
    edge_sizes = jax.random.randint(key_edge, (owner_count - 1,), 1, largest + 1)
    edge_signs = jnp.where(jax.random.permutation(key_sign, owner_count - 1) < (owner_count - 1) // 2, -1, 1)
    chosen_edges = jax.random.permutation(key_pick, owner_count - 1)
    rising = chosen_edges[0]
    falling = chosen_edges[1]
    edge_sizes = edge_sizes.at[rising].set(largest).at[falling].set(largest)
    edge_signs = edge_signs.at[rising].set(1).at[falling].set(-1)
    edge_places = (jnp.arange(owner_count - 1, dtype=jnp.int32) + 1) * members - 1
    drifts = inner.at[edge_places].set(edge_signs * edge_sizes)
    drifts = drifts.at[(rising + 1) * members - 2].set(-quarter)
    drifts = drifts.at[NDEV - 1].set(0)
    earlier = jnp.concatenate([jnp.zeros((1,), jnp.int32), drifts[:-1]])
    counts = SPAN_DEV + drifts - earlier
    orders = jax.vmap(lambda single: jax.random.permutation(single, BYTES_DEV))(jax.random.split(key_order, NDEV))
    column = jnp.arange(BYTES_DEV)
    leading = orders[0]
    moved = jnp.where(column == 0, 0, jnp.where(leading < leading[0], leading + 1, leading))
    orders = orders.at[0].set(moved)
    flags = orders < counts[:, None]
    return jnp.nonzero(flags.reshape(-1), size=SPANS)[0].astype(jnp.int32)


def block_levels(rng, dims, shards, low, top_value):
    def one(axis_at, parts):
        draws = jax.random.uniform(jax.random.fold_in(jax.random.fold_in(rng, 6), axis_at), (parts,), jnp.float32, low / len(shards), top_value / len(shards))
        return jnp.repeat(jnp.exp(draws), dims[axis_at] // parts).reshape((-1,) + (1,) * (len(dims) - axis_at - 1))

    loudness = one(*shards[0])
    for cut in shards[1:]:
        loudness = loudness * one(*cut)
    return loudness


def noise(key, shape, scale, most, pieces=(), kind=jnp.bfloat16):
    drawn = jax.random.normal(key, shape, jnp.float32) * scale
    if len(pieces) > 0:
        drawn = block_levels(key, shape, pieces, -0.22, 0.18) * drawn
    return jnp.clip(drawn, min=-most, max=most).astype(kind)


def setup_inputs(seed: int = 0, part: int = 0) -> dict:
    arg_keys = jax.random.split(jax.random.key(seed), 12)
    own_keys = jax.random.split(jax.random.fold_in(arg_keys[11], part), 12)
    byte_states = draw_byte_states(jax.random.fold_in(jax.random.fold_in(arg_keys[11], part), 71), part)
    cotangent = noise(own_keys[1], (SEQ_LEN, E), 1.0, 6.0, ((0, 16),))
    boundaries = draw_boundaries(jax.random.fold_in(jax.random.fold_in(arg_keys[11], part), 71), part)
    enc_gain = jnp.clip(1.0 + 0.15 * jax.random.normal(arg_keys[3], (E,), jnp.float32), 0.25, 1.75)
    w_qkv = draw_w_qkv(jax.random.fold_in(arg_keys[11], 71), part)
    w_out = noise(arg_keys[5], (E, E), E ** -0.5, 0.1875)
    pad_vector = noise(arg_keys[6], (D - E,), 1.0, 5.0, (), jnp.float32)
    main_gain = jnp.clip(1.0 + 0.15 * jax.random.normal(arg_keys[7], (D,), jnp.float32), 0.25, 1.75)
    gate_w = noise(arg_keys[8], (D, FF), D ** -0.5, 0.09375, ((0, 4), (1, 4)))
    up_w = noise(arg_keys[9], (D, FF), D ** -0.5, 0.09375, ((0, 4), (1, 4)))
    down_t = noise(arg_keys[10], (D, FF), FF ** -0.5, 0.078125, ((0, 4), (1, 4)))
    return dict(byte_states=byte_states, cotangent=cotangent, boundaries=boundaries, enc_gain=enc_gain, w_qkv=w_qkv, w_out=w_out, pad_vector=pad_vector, main_gain=main_gain, gate_w=gate_w, up_w=up_w, down_t=down_t)


def rms_scale(values, gain):
    return values * lax.rsqrt(lax.optimization_barrier(jnp.mean(values * values, axis=-1, keepdims=True)) + 1e-05) * gain

def reference(byte_states, cotangent, boundaries, enc_gain, w_qkv, w_out, pad_vector, main_gain, gate_w, up_w, down_t):
    x_float = byte_states.astype(jnp.float32)
    normed = rms_scale(x_float, enc_gain).astype(jnp.bfloat16)
    qkv = jnp.dot(normed, w_qkv, preferred_element_type=jnp.float32).astype(jnp.bfloat16)
    queries = qkv[:, :E]
    padded_kv = jnp.concatenate([jnp.zeros((WINDOW, 2 * E), jnp.bfloat16), qkv[:, E:]], axis=0)
    n_blocks = SEQ_LEN // BYTES_DEV

    def one_block(block):
        begin = (block * BYTES_DEV).astype(jnp.int32)
        query_rows = lax.dynamic_slice(queries, (begin, jnp.int32(0)), (BYTES_DEV, E))
        key_rows = lax.dynamic_slice(padded_kv, (begin, jnp.int32(0)), (WINDOW + BYTES_DEV, 2 * E))
        qpos = begin + jnp.arange(BYTES_DEV, dtype=jnp.int32)
        kpos = begin - WINDOW + jnp.arange(WINDOW + BYTES_DEV, dtype=jnp.int32)
        allowed = (kpos[None, :] <= qpos[:, None]) & (kpos[None, :] > qpos[:, None] - WINDOW) & (kpos[None, :] >= 0)
        q_heads = query_rows.reshape(BYTES_DEV, HEADS, HEAD).astype(jnp.float32)
        k_heads = key_rows[:, :E].reshape(WINDOW + BYTES_DEV, HEADS, HEAD).astype(jnp.float32)
        v_heads = key_rows[:, E:].reshape(WINDOW + BYTES_DEV, HEADS, HEAD).astype(jnp.float32)
        scores = jnp.einsum('qhd,khd->hqk', q_heads, k_heads) / jnp.sqrt(jnp.float32(HEAD))
        scores = jnp.where(allowed[None], scores, jnp.float32(-1e+30))
        probs = jax.nn.softmax(scores, axis=-1).astype(jnp.bfloat16)
        mixed = jnp.einsum('hqk,khd->qhd', probs.astype(jnp.float32), v_heads)
        return mixed.reshape(BYTES_DEV, E).astype(jnp.bfloat16)
    attended = lax.map(one_block, jnp.arange(n_blocks, dtype=jnp.int32)).reshape(SEQ_LEN, E)
    encoded = (x_float + jnp.dot(attended, w_out, preferred_element_type=jnp.float32)).astype(jnp.bfloat16)
    positions = jnp.arange(SEQ_LEN, dtype=jnp.int32)
    span_index = (jnp.searchsorted(boundaries, positions, side='right') - 1).astype(jnp.int32)
    start_block = (boundaries[span_index] // BYTES_DEV).astype(jnp.int32)
    piece_index = (positions // BYTES_DEV - start_block).astype(jnp.int32)
    segment = span_index * 2 + piece_index
    piece_sum = jax.ops.segment_sum(cotangent.astype(jnp.float32), segment, num_segments=2 * SPANS).astype(jnp.bfloat16)
    span_grad = lax.optimization_barrier(jnp.sum(piece_sum.astype(jnp.float32).reshape(SPANS, 2, E), axis=1)).astype(jnp.bfloat16)
    rows = encoded[boundaries].astype(jnp.float32)
    wide = jnp.concatenate([rows, jnp.broadcast_to(pad_vector, (SPANS, D - E))], axis=1)
    main_in = rms_scale(wide, main_gain).astype(jnp.bfloat16)
    gate = jnp.dot(main_in, gate_w, preferred_element_type=jnp.float32)
    upward = jnp.dot(main_in, up_w, preferred_element_type=jnp.float32)
    hidden = (jax.nn.silu(gate) * upward).astype(jnp.bfloat16)
    output = lax.dot_general(hidden, down_t, (((1,), (1,)), ((), ())), preferred_element_type=jnp.float32)
    main_out = (wide + output).astype(jnp.bfloat16)
    return (main_out, span_grad)
```

```python
import jax
import jax.numpy as jnp
from jax import lax
from jax.sharding import PartitionSpec as P

HEAD = 128
WINDOW = 128
CAP = 64
LANE = 24
PART = ("seq", "mp", "rep")
MEMBER = ("mp", "rep")
F32 = jnp.float32
BF16 = jnp.bfloat16


def dot(a, b):
    return jnp.dot(a, b, preferred_element_type=F32)


def dot_t(a, b):
    return lax.dot_general(a, b, (((1,), (1,)), ((), ())), preferred_element_type=F32)


def rms_scale(values, gain):
    return values * lax.rsqrt(jnp.mean(values * values, axis=-1, keepdims=True) + 1e-05) * gain


def encode(x, halo, begin, sel, q_at, enc_gain, w_qkv, w_out):
    length, width = x.shape
    heads = width // HEAD
    both = jnp.concatenate([halo, x], axis=0)
    normed = rms_scale(both.astype(F32), enc_gain).astype(BF16)
    picked = dot(sel, normed[length:]).astype(BF16)
    queries = dot(picked, w_qkv[:, :width]).astype(BF16)
    keyval = dot(normed, w_qkv[:, width:]).astype(BF16)
    k_at = jnp.arange(2 * length, dtype=jnp.int32) - length
    allowed = (
        (k_at[None, :] <= q_at[:, None])
        & (k_at[None, :] > q_at[:, None] - WINDOW)
        & (k_at[None, :] + begin >= 0)
    )
    q_heads = queries.reshape(CAP, heads, HEAD)
    k_heads = keyval[:, :width].reshape(2 * length, heads, HEAD)
    v_heads = keyval[:, width:].reshape(2 * length, heads, HEAD)
    scores = jnp.einsum("qhd,khd->hqk", q_heads, k_heads, preferred_element_type=F32)
    scores = jnp.where(allowed[None], scores / jnp.sqrt(F32(HEAD)), F32(-1e30))
    probs = jax.nn.softmax(scores, axis=-1).astype(BF16)
    mixed = jnp.einsum("hqk,khd->qhd", probs, v_heads, preferred_element_type=F32)
    attended = mixed.reshape(CAP, width).astype(BF16)
    return (dot(sel, x) + dot(attended, w_out)).astype(BF16)


def sum_of_spans(cotangent, span_index):
    n_member = lax.axis_size(MEMBER)
    n_seq = lax.axis_size("seq")
    owner = lax.axis_index("seq")
    length, width = cotangent.shape
    span_own = 32 * n_member
    lowest, highest = span_index[0], span_index[length - 1]
    slot_ids = jnp.arange(CAP, dtype=jnp.int32)
    onehot = (span_index[None, :] - lowest == slot_ids[:, None]).astype(BF16)
    pieces = dot(onehot, cotangent).astype(BF16)
    span_ids = lowest + slot_ids
    valid = (span_ids <= highest)[None, :]
    lane_ids = jnp.arange(LANE, dtype=jnp.int32)
    row_ids = jnp.arange(span_own, dtype=jnp.int32)

    def choose(targets):
        return dot(((targets[:, None] == span_ids[None, :]) & valid).astype(BF16), pieces)

    to_before = choose(owner * span_own - LANE + lane_ids).astype(BF16)
    to_after = choose((owner + 1) * span_own + lane_ids).astype(BF16)
    up = [(i, i + 1) for i in range(n_seq - 1)]
    down = [(i + 1, i) for i in range(n_seq - 1)]
    from_before = lax.ppermute(to_after, "seq", up).astype(F32)
    from_after = lax.ppermute(to_before, "seq", down).astype(F32)
    block = choose(owner * span_own + row_ids)
    block = jnp.concatenate(
        [block[:LANE] + from_before, block[LANE:-LANE], block[-LANE:] + from_after], axis=0
    )
    sent = block.astype(BF16).reshape(n_member, span_own // n_member, width)
    got = lax.all_to_all(sent, MEMBER, 0, 0, tiled=True)
    return jnp.sum(got.astype(F32), axis=0).astype(BF16)


def split_high_low(values):
    high = values.astype(BF16)
    return high, (values - high.astype(F32)).astype(BF16)


def local(
    byte_states,
    cotangent,
    boundaries,
    enc_gain,
    w_qkv,
    w_out,
    pad_vector,
    main_gain,
    gate_w,
    up_w,
    down_t,
):
    n_member = lax.axis_size(MEMBER)
    n_seq = lax.axis_size("seq")
    n_dev = n_seq * n_member
    seq = lax.axis_index("seq")
    device = lax.axis_index(PART)
    length, width = byte_states.shape
    depth, columns = gate_w.shape
    main_width = depth * n_seq
    n_span = boundaries.shape[0]
    share = n_span // n_dev
    begin = device * length

    shift = [(i, i + 1) for i in range(n_dev - 1)]
    halo = lax.ppermute(byte_states, PART, shift)

    wide_gain = main_gain[width:]
    pad_in = jnp.concatenate([jnp.zeros((width,), F32), pad_vector * wide_gain])
    pad_here = lax.dynamic_slice_in_dim(pad_in, seq * depth, depth, 0)
    pad_rows = jnp.stack(split_high_low(pad_here) * 4)
    pad_terms = jnp.concatenate([dot(pad_rows, gate_w), dot(pad_rows, up_w)], axis=1)
    pad_terms = pad_terms[:1] + pad_terms[1:2]

    places = jnp.arange(length, dtype=jnp.int32)
    earlier = jnp.sum((boundaries[:, None] < begin + places[None, :]).astype(jnp.int32), axis=0)
    starts = jnp.sum((boundaries[:, None] == begin + places[None, :]).astype(jnp.int32), axis=0)
    slot_ids = jnp.arange(CAP, dtype=jnp.int32)
    picks = (earlier - earlier[0] == slot_ids[:, None]) & (starts > 0)
    q_at = jnp.sum(jnp.where(picks, places[None, :], 0), axis=1)
    sel = picks.astype(BF16)
    blocks = jnp.arange(n_dev, dtype=jnp.int32)
    block_first = jnp.sum((boundaries[:, None] < blocks[None, :] * length).astype(jnp.int32), axis=0)
    block_count = jnp.concatenate([block_first[1:], jnp.full((1,), n_span, jnp.int32)]) - block_first
    span_at = jnp.where(
        slot_ids[None, :] < block_count[:, None], block_first[:, None] + slot_ids[None, :], -1
    )

    span_grad = sum_of_spans(cotangent, earlier + starts - 1)
    rows = encode(byte_states, halo, begin, sel, q_at, enc_gain, w_qkv, w_out)

    gain_rows = main_gain[:width]
    order = jnp.arange(n_span, dtype=jnp.int32).reshape(n_seq, n_member, share)
    order = order.transpose(1, 0, 2).reshape(-1)
    direct = depth == width and n_seq == 4
    if direct:
        others = [lax.ppermute(rows, "seq", [(j, 0)]) for j in range(1, n_seq)]
        column = jnp.stack([rows] + others)
        gathered = lax.all_gather(column, MEMBER, axis=0)
        gathered = gathered.reshape(n_dev * CAP, width)
        row_span = span_at.reshape(n_seq, n_member, CAP).transpose(1, 0, 2).reshape(-1)
    else:
        gathered = lax.all_gather(rows, PART, axis=0, tiled=True)
        row_span = span_at.reshape(-1)
    compact = dot((order[:, None] == row_span[None, :]).astype(BF16), gathered)
    squares = jnp.sum(compact * compact, axis=1, keepdims=True) + jnp.sum(pad_vector * pad_vector)
    scale = lax.rsqrt(squares / main_width + 1e-05)
    main_in = (compact * scale * gain_rows).astype(BF16)

    if direct:
        pad_sum = pad_terms
        for j in range(1, n_seq):
            pad_sum = pad_sum + lax.ppermute(pad_terms, "seq", [(j, 0)])
        gate = dot(main_in, gate_w) + scale * pad_sum[:, :columns]
        upward = dot(main_in, up_w) + scale * pad_sum[:, columns:]
        hidden = (jax.nn.silu(gate) * upward).astype(BF16)
        at_two = lax.ppermute(hidden, "seq", [(0, 2)])
        at_one = lax.ppermute(at_two, "seq", [(2, 1)])
        at_three = lax.ppermute(at_two, "seq", [(2, 3)])
        hidden = jnp.where(
            seq == 0, hidden, jnp.where(seq == 2, at_two, jnp.where(seq == 1, at_one, at_three))
        )
    else:
        padded = jnp.pad(main_in, ((0, 0), (0, main_width - width)))
        here = lax.dynamic_slice_in_dim(padded, seq * depth, depth, 1)
        gate = dot(here, gate_w) + scale * pad_terms[:, :columns]
        upward = dot(here, up_w) + scale * pad_terms[:, columns:]
        gate, upward = lax.psum((gate, upward), "seq")
        hidden = (jax.nn.silu(gate) * upward).astype(BF16)

    partial = dot_t(hidden, down_t).astype(BF16).reshape(n_member, n_seq * share, depth)
    got = lax.all_to_all(partial, MEMBER, 0, 0, tiled=True)
    summed = jnp.sum(got.astype(F32), axis=0)
    member = lax.axis_index(MEMBER)
    mine = lax.dynamic_slice_in_dim(compact, member * n_seq * share, n_seq * share, 0)
    wide = jnp.concatenate(
        [mine, jnp.broadcast_to(pad_vector, (n_seq * share, main_width - width))], axis=1
    )
    residual = lax.dynamic_slice_in_dim(wide, seq * depth, depth, 1)
    done = (summed + residual).astype(BF16).reshape(n_seq, share, depth)
    spread = lax.all_to_all(done, "seq", 0, 0, tiled=True)
    main_out = spread.transpose(1, 0, 2).reshape(share, main_width)
    return (main_out, span_grad)


def solution(mesh):
    spread = P(("groups", "seq", "mp", "rep"), None)
    weight = P("seq", ("mp", "rep"))
    placed = (spread, spread, P("groups"), P(), P(), P(), P(), P(), weight, weight, weight)
    return jax.shard_map(
        local, mesh=mesh, in_specs=placed, out_specs=(spread, spread), check_vma=False
    )
```

```python
import jax
import jax.numpy as jnp
from jax import lax
from jax.experimental import pallas as pl
from jax.experimental.pallas import tpu as pltpu
from jax.sharding import PartitionSpec as P

HEAD = 128
WINDOW = 128
CAP = 64
LANE = 24
LANE_ROWS = 32
HALF = 96
VMEM_LIMIT = 56 << 20
CHUNKS = ((0, (0, 1, 2)), (1, (3, 4, 5, 6)), (2, (7, 8, 9, 10)), (3, (11, 12, 13)), (3, (14, 15)))
PART = ("seq", "mp", "rep")
MEMBER = ("mp", "rep")
F32 = jnp.float32
BF16 = jnp.bfloat16


def dot(a, b):
    return jnp.dot(a, b, preferred_element_type=F32)


def dot_t(a, b):
    return lax.dot_general(a, b, (((1,), (1,)), ((), ())), preferred_element_type=F32)


def is_direct():
    return lax.axis_size("seq") == 4 and lax.axis_size("mp") == 2 and lax.axis_size("rep") == 2


def swap(value, axis):
    return lax.ppermute(value, axis, [(0, 1), (1, 0)])


def pick(index, values):
    out = values[-1]
    for i in range(len(values) - 2, -1, -1):
        out = jnp.where(index == i, values[i], out)
    return out


def sum_members(value):
    mp, rep = lax.axis_index("mp"), lax.axis_index("rep")
    rows = value.reshape((2, 2) + value.shape[1:])
    keep = pick(rep, [rows[:, 0], rows[:, 1]])
    send = pick(rep, [rows[:, 1], rows[:, 0]])
    keep = keep + swap(send.astype(BF16), "rep").astype(F32)
    own = pick(mp, [keep[0], keep[1]])
    other = pick(mp, [keep[1], keep[0]])
    return own + swap(other.astype(BF16), "mp").astype(F32)


def rms_scale(values, gain):
    return values * lax.rsqrt(jnp.mean(values * values, axis=-1, keepdims=True) + 1e-05) * gain


def encode(x, halo, begin, sel, q_at, enc_gain, w_qkv, w_out):
    length, width = x.shape
    heads = width // HEAD
    both = jnp.concatenate([halo, x], axis=0)
    normed = rms_scale(both.astype(F32), enc_gain).astype(BF16)
    picked = dot(sel, normed[length:]).astype(BF16)
    queries = dot(picked, w_qkv[:, :width]).astype(BF16)
    keyval = dot(normed, w_qkv[:, width:]).astype(BF16)
    k_at = jnp.arange(2 * length, dtype=jnp.int32) - length
    allowed = (
        (k_at[None, :] <= q_at[:, None])
        & (k_at[None, :] > q_at[:, None] - WINDOW)
        & (k_at[None, :] + begin >= 0)
    )
    q_heads = queries.reshape(CAP, heads, HEAD)
    k_heads = keyval[:, :width].reshape(2 * length, heads, HEAD)
    v_heads = keyval[:, width:].reshape(2 * length, heads, HEAD)
    scores = jnp.einsum("qhd,khd->hqk", q_heads, k_heads, preferred_element_type=F32)
    scores = jnp.where(allowed[None], scores / jnp.sqrt(F32(HEAD)), F32(-1e30))
    probs = jax.nn.softmax(scores, axis=-1).astype(BF16)
    mixed = jnp.einsum("hqk,khd->qhd", probs, v_heads, preferred_element_type=F32)
    attended = mixed.reshape(CAP, width).astype(BF16)
    return (dot(sel, x) + dot(attended, w_out)).astype(BF16)


def sum_of_spans(cotangent, span_index):
    n_member = lax.axis_size(MEMBER)
    n_seq = lax.axis_size("seq")
    owner = lax.axis_index("seq")
    length, width = cotangent.shape
    span_own = 32 * n_member
    lowest, highest = span_index[0], span_index[length - 1]
    slot_ids = jnp.arange(CAP, dtype=jnp.int32)
    onehot = (span_index[None, :] - lowest == slot_ids[:, None]).astype(BF16)
    pieces = dot(onehot, cotangent).astype(BF16)
    span_ids = lowest + slot_ids
    valid = (span_ids <= highest)[None, :]
    lane_ids = jnp.arange(LANE, dtype=jnp.int32)
    row_ids = jnp.arange(span_own, dtype=jnp.int32)

    def choose(targets):
        return dot(((targets[:, None] == span_ids[None, :]) & valid).astype(BF16), pieces)

    to_before = choose(owner * span_own - LANE + lane_ids).astype(BF16)
    to_after = choose((owner + 1) * span_own + lane_ids).astype(BF16)
    up = [(i, i + 1) for i in range(n_seq - 1)]
    down = [(i + 1, i) for i in range(n_seq - 1)]
    from_before = lax.ppermute(to_after, "seq", up).astype(F32)
    from_after = lax.ppermute(to_before, "seq", down).astype(F32)
    block = choose(owner * span_own + row_ids)
    block = jnp.concatenate(
        [block[:LANE] + from_before, block[LANE:-LANE], block[-LANE:] + from_after], axis=0
    )
    sent = block.astype(BF16).reshape(n_member, span_own // n_member, width)
    got = lax.all_to_all(sent, MEMBER, 0, 0, tiled=True)
    return jnp.sum(got.astype(F32), axis=0).astype(BF16)


def relay(value):
    return lax.ppermute(value, "seq", [(2, 1)]), lax.ppermute(value, "seq", [(2, 3)])


def exchange_sums(sums):
    own = sums.shape[0] - 2 * LANE_ROWS
    n_seq = lax.axis_size("seq")
    up = [(i, i + 1) for i in range(n_seq - 1)]
    down = [(i + 1, i) for i in range(n_seq - 1)]
    from_after = lax.ppermute(sums[own : own + LANE_ROWS], "seq", down)
    from_before = lax.ppermute(sums[own + LANE_ROWS :], "seq", up)
    return from_before, from_after


def route_sums(sums, from_both):
    own = sums.shape[0] - 2 * LANE_ROWS
    first, last = (value.astype(F32) for value in from_both)
    block = sums[:own].astype(F32)
    block = jnp.concatenate(
        [block[:LANE_ROWS] + first, block[LANE_ROWS:-LANE_ROWS], block[-LANE_ROWS:] + last], axis=0
    )
    return sum_members(block.reshape(4, own // 4, -1)).astype(BF16)


def pad_kernel(at_ref, pad_ref, gain_ref, gate_ref, up_ref, out_ref):
    high, low = split_high_low(jnp.broadcast_to(pad_ref[...] * gain_ref[...], (8, pad_ref.shape[1])))
    both = jnp.concatenate([high, low], axis=0)
    for at, weight_ref in enumerate((gate_ref, up_ref)):
        terms = dot(both, weight_ref[...])
        terms = terms[:1] + terms[8:9]
        out_ref[at : at + 1] = jnp.where(at_ref[2] == 0, 0.0, terms)


def pad_terms_of(at, pad_vector, main_gain, gate_w, up_w):
    depth, columns = gate_w.shape
    block = 4 * HEAD
    pad_block = pl.BlockSpec((1, depth), lambda i, at: (0, jnp.maximum(at[2] - 1, 0)))
    gain_block = pl.BlockSpec((1, depth), lambda i, at: (0, at[2]))
    weight_block = pl.BlockSpec((depth, block), lambda i, at: (0, i))
    return pl.pallas_call(
        pad_kernel,
        out_shape=jax.ShapeDtypeStruct((2, columns), F32),
        grid_spec=pltpu.PrefetchScalarGridSpec(
            num_scalar_prefetch=1,
            grid=(columns // block,),
            in_specs=[pad_block, gain_block, weight_block, weight_block],
            out_specs=pl.BlockSpec((2, block), lambda i, at: (0, i)),
        ),
        compiler_params=pltpu.CompilerParams(vmem_limit_bytes=VMEM_LIMIT),
        cost_estimate=pl.CostEstimate(flops=100_000_000, bytes_accessed=6_500_000, transcendentals=0),
        name="pad_terms",
    )(at, pad_vector.reshape(1, -1), main_gain.reshape(1, -1), gate_w, up_w)


def plan_kernel(at_ref, starts_ref, cotangent_ref, sel_ref, bias_ref, pack_ref, place_ref, sums_ref):
    device, member, owner = at_ref[0], at_ref[1], at_ref[2]
    n_span = starts_ref.shape[1]
    length = cotangent_ref.shape[0]
    begin = device * length
    row = starts_ref[...]
    column = jnp.transpose(jnp.broadcast_to(row, (length, n_span)))
    here = begin + lax.broadcasted_iota(jnp.int32, (n_span, length), 1)
    earlier = jnp.sum(jnp.where(column < here, 1.0, 0.0), axis=0, keepdims=True).astype(jnp.int32)
    start = jnp.sum(jnp.where(column == here, 1.0, 0.0), axis=0, keepdims=True).astype(jnp.int32)
    slot = lax.broadcasted_iota(jnp.int32, (CAP, length), 0)
    picked = (earlier - earlier[:, :1] == slot) & (start > 0)
    picked = jnp.where(picked, 1.0, 0.0)
    sel_ref[...] = picked.astype(BF16)
    place_in = lax.broadcasted_iota(jnp.int32, (CAP, length), 1).astype(F32)
    q_at = jnp.sum(picked * place_in, axis=1, keepdims=True).astype(jnp.int32)
    k_at = lax.broadcasted_iota(jnp.int32, (CAP, 2 * length), 1) - length
    allowed = (k_at <= q_at) & (k_at > q_at - WINDOW) & (k_at + begin >= 0)
    bias_ref[...] = jnp.where(allowed, 0.0, -1e30)

    span_index = earlier + start - 1
    n_row = sums_ref.shape[0]
    own = n_row - 2 * LANE_ROWS
    at = lax.broadcasted_iota(jnp.int32, (n_row, length), 0)
    target = jnp.where(
        at < own, owner * own + at, jnp.where(at < own + LANE_ROWS, owner * own - LANE_ROWS - own, owner * own - LANE_ROWS) + at
    )
    member_of = jnp.where(span_index == target, 1.0, 0.0).astype(BF16)
    sums_ref[...] = dot(member_of, cotangent_ref[...]).astype(BF16)

    block = owner * 4 + lax.broadcasted_iota(jnp.int32, (n_span, 4 * CAP), 1) // CAP
    first = jnp.sum(jnp.where(column[:, :1] < block * length, 1.0, 0.0), axis=0, keepdims=True).astype(jnp.int32)
    next_first = jnp.sum(jnp.where(column[:, :1] < block * length + length, 1.0, 0.0), axis=0, keepdims=True).astype(jnp.int32)
    lane = lax.broadcasted_iota(jnp.int32, (2 * HALF, 4 * CAP), 1) % CAP
    held = lax.broadcasted_iota(jnp.int32, (2 * HALF, 4 * CAP), 0) + first[:, :1]
    pack_ref[...] = jnp.where((first + lane == held) & (held < next_first), 1.0, 0.0).astype(BF16)

    around = column[:, :1] // (4 * length)
    before = jnp.sum(jnp.where(row < around * (4 * length), 1.0, 0.0), axis=1, keepdims=True).astype(jnp.int32)
    span = lax.broadcasted_iota(jnp.int32, (n_span, 1), 0)
    near = jnp.minimum((span // 32 + 1) // 4, 3)
    lies = span - before
    side = jnp.where(lies >= HALF, 1, 0)
    lies = lies - side * HALF + (side ^ (member % 2)) * HALF + (around - near + 1) * (2 * HALF)
    lanes = lax.broadcasted_iota(jnp.int32, place_ref.shape, 1)
    place_ref[...] = jnp.where(lanes == lies, 1.0, 0.0).astype(BF16)


def plan(at, boundaries, cotangent, span_own):
    n_span = boundaries.shape[0]
    length, width = cotangent.shape
    shapes = ((CAP, length), (CAP, 2 * length), (2 * HALF, 4 * CAP), (n_span, 4 * HALF), (span_own + 2 * LANE_ROWS, width))
    return pl.pallas_call(
        plan_kernel,
        out_shape=tuple(jax.ShapeDtypeStruct(s, F32 if i == 1 else BF16) for i, s in enumerate(shapes)),
        in_specs=[
            pl.BlockSpec(memory_space=pltpu.SMEM),
            pl.BlockSpec(memory_space=pltpu.VMEM),
            pl.BlockSpec(memory_space=pltpu.VMEM),
        ],
        out_specs=tuple(pl.BlockSpec(memory_space=pltpu.VMEM) for _ in shapes),
        compiler_params=pltpu.CompilerParams(vmem_limit_bytes=16 << 20),
        cost_estimate=pl.CostEstimate(flops=60_000_000, bytes_accessed=1_500_000, transcendentals=0),
        name="plan",
    )(at, boundaries.reshape(1, n_span), cotangent)


def encode_kernel(x_ref, halo_ref, sel_ref, bias_ref, gain_ref, qkv_ref, o_ref, out_ref):
    length, width = x_ref.shape
    gain = gain_ref[...]
    sel = sel_ref[...]
    bias = bias_ref[...]
    normed = rms_scale(x_ref[...].astype(F32), gain).astype(BF16)
    picked = dot(sel, normed).astype(BF16)
    normed = jnp.concatenate([rms_scale(halo_ref[...].astype(F32), gain).astype(BF16), normed], axis=0)
    mixed = []
    wide = 2 * HEAD
    for at in range(0, width, wide):
        queries = dot(picked, qkv_ref[:, at : at + wide]).astype(BF16)
        keys = dot(normed, qkv_ref[:, width + at : width + at + wide]).astype(BF16)
        values = dot(normed, qkv_ref[:, 2 * width + at : 2 * width + at + wide]).astype(BF16)
        for head in range(0, wide, HEAD):
            part = slice(head, head + HEAD)
            scores = dot_t(queries[:, part], keys[:, part]) * (HEAD**-0.5) + bias
            probs = jnp.exp(scores - jnp.max(scores, axis=1, keepdims=True))
            probs = (probs / jnp.sum(probs, axis=1, keepdims=True)).astype(BF16)
            mixed.append(dot(probs, values[:, part]).astype(BF16))
    total = dot(sel, x_ref[...]) + dot(jnp.concatenate(mixed, axis=1), o_ref[...])
    out_ref[...] = total.astype(BF16)


def encode_direct(x, halo, sel, bias, enc_gain, w_qkv, w_out):
    length, width = x.shape
    return pl.pallas_call(
        encode_kernel,
        out_shape=jax.ShapeDtypeStruct((CAP, width), BF16),
        in_specs=[pl.BlockSpec(memory_space=pltpu.VMEM)] * 7,
        out_specs=pl.BlockSpec(memory_space=pltpu.VMEM),
        compiler_params=pltpu.CompilerParams(vmem_limit_bytes=32 << 20),
        cost_estimate=pl.CostEstimate(flops=1_500_000_000, bytes_accessed=9_000_000, transcendentals=200_000),
        name="encode",
    )(x, halo, sel, bias, enc_gain.reshape(1, width), w_qkv, w_out)


def split_high_low(values):
    high = values.astype(BF16)
    return high, (values - high.astype(F32)).astype(BF16)


def block_first(boundaries, blocks, length):
    edges = jnp.stack([blocks, blocks + 1]) * length
    return jnp.sum((boundaries[:, None, None] < edges[None]).astype(jnp.int32), axis=0)


def place(first, span_ids):
    slots = jnp.arange(CAP, dtype=jnp.int32)
    held = first[0][:, None] + slots[None, :]
    held = jnp.where(held < first[1][:, None], held, -1).reshape(-1)
    return (span_ids[:, None] == held[None, :]).astype(BF16)


def local(
    byte_states,
    cotangent,
    boundaries,
    enc_gain,
    w_qkv,
    w_out,
    pad_vector,
    main_gain,
    gate_w,
    up_w,
    down_t,
):
    n_member = lax.axis_size(MEMBER)
    n_seq = lax.axis_size("seq")
    n_dev = n_seq * n_member
    seq = lax.axis_index("seq")
    device = lax.axis_index(PART)
    length, width = byte_states.shape
    depth, columns = gate_w.shape
    main_width = depth * n_seq
    n_span = boundaries.shape[0]
    share = n_span // n_dev
    begin = device * length

    shift = [(i, i + 1) for i in range(n_dev - 1)]
    halo = lax.ppermute(byte_states, PART, shift)

    direct = is_direct() and depth == width
    if direct:
        same_seq = swap(jnp.full((8, 128), seq, jnp.int32), "rep")[0, 0]
        at = jnp.stack([device, lax.axis_index(MEMBER), same_seq]).astype(jnp.int32)
        pad_terms = pad_terms_of(at, pad_vector, main_gain, gate_w, up_w)
        sel, bias, pack, where, sums = plan(at, boundaries, cotangent, n_member * share)
        rows = encode_direct(byte_states, halo, sel, bias, enc_gain, w_qkv, w_out)
    else:
        wide_gain = main_gain[width:]
        pad_in = jnp.concatenate([jnp.zeros((width,), F32), pad_vector * wide_gain])
        pad_here = lax.dynamic_slice_in_dim(pad_in, seq * depth, depth, 0)
        pad_rows = jnp.stack(split_high_low(pad_here) * 4)
        pad_terms = jnp.concatenate([dot(pad_rows, gate_w), dot(pad_rows, up_w)], axis=1)
        pad_terms = pad_terms[:1] + pad_terms[1:2]

        places = jnp.arange(length, dtype=jnp.int32)
        earlier = jnp.sum((boundaries[:, None] < begin + places[None, :]).astype(jnp.int32), axis=0)
        starts = jnp.sum((boundaries[:, None] == begin + places[None, :]).astype(jnp.int32), axis=0)
        slot_ids = jnp.arange(CAP, dtype=jnp.int32)
        picks = (earlier - earlier[0] == slot_ids[:, None]) & (starts > 0)
        q_at = jnp.sum(jnp.where(picks, places[None, :], 0), axis=1)
        sel = picks.astype(BF16)
        span_grad = sum_of_spans(cotangent, earlier + starts - 1)
        rows = encode(byte_states, halo, begin, sel, q_at, enc_gain, w_qkv, w_out)

    gain_rows = main_gain[:width]
    pad_square = jnp.sum(pad_vector * pad_vector)

    def scaled(compact):
        squares = jnp.sum(compact * compact, axis=1, keepdims=True) + pad_square
        scale = lax.rsqrt(squares / main_width + 1e-05)
        return scale, (compact * scale * gain_rows).astype(BF16)

    if not direct:
        gathered = lax.all_gather(rows, PART, axis=0, tiled=True)
        order = jnp.arange(n_span, dtype=jnp.int32).reshape(n_seq, n_member, share)
        order = order.transpose(1, 0, 2).reshape(-1)
        first = block_first(boundaries, jnp.arange(n_dev, dtype=jnp.int32), length)
        compact = dot(place(first, order), gathered)
        scale, main_in = scaled(compact)
        padded = jnp.pad(main_in, ((0, 0), (0, main_width - width)))
        here = lax.dynamic_slice_in_dim(padded, seq * depth, depth, 1)
        gate = dot(here, gate_w) + scale * pad_terms[:, :columns]
        upward = dot(here, up_w) + scale * pad_terms[:, columns:]
        gate, upward = lax.psum((gate, upward), "seq")
        hidden = (jax.nn.silu(gate) * upward).astype(BF16)
        partial = dot_t(hidden, down_t).astype(BF16).reshape(n_member, n_seq * share, depth)
        got = lax.all_to_all(partial, MEMBER, 0, 0, tiled=True)
        summed = jnp.sum(got.astype(F32), axis=0)
        member = lax.axis_index(MEMBER)
        mine = lax.dynamic_slice_in_dim(compact, member * n_seq * share, n_seq * share, 0)
        wide = jnp.concatenate(
            [mine, jnp.broadcast_to(pad_vector, (n_seq * share, main_width - width))], axis=1
        )
        residual = lax.dynamic_slice_in_dim(wide, seq * depth, depth, 1)
        done = (summed + residual).astype(BF16).reshape(n_seq, share, depth)
        spread = lax.all_to_all(done, "seq", 0, 0, tiled=True)
        main_out = spread.transpose(1, 0, 2).reshape(share, main_width)
        return (main_out, span_grad)

    pad_parts = [lax.ppermute(pad_terms, "seq", [(j, 0)]) for j in range(1, n_seq)]

    member = lax.axis_index(MEMBER)
    core = lax.axis_index("rep")
    packed = dot(pack, lax.all_gather(rows, MEMBER, axis=0, tiled=True)).astype(BF16)
    packed, pad_parts = lax.optimization_barrier((packed, pad_parts))
    pad_gate, pad_up = sum(pad_parts)[:1], sum(pad_parts)[1:]
    halves = [packed[:HALF], packed[HALF:]]
    mine = jnp.where(core == 0, halves[0], halves[1])
    came = [mine] + [lax.ppermute(mine, "seq", [(j, 0)]) for j in range(1, n_seq)]
    planes = [jnp.concatenate([mine, jnp.where(core == 0, halves[1], halves[0])], axis=0)]

    worked, kept, relayed, spread = [], [], [], []
    for index, (near, groups) in enumerate(CHUNKS):
        while len(planes) <= near:
            value, kept[-1] = lax.optimization_barrier((came[len(planes)], kept[-1]))
            planes.append(jnp.concatenate([value, swap(value, "rep")], axis=0))
        low = groups[0] * share
        high = low + len(groups) * share
        if near:
            compact = dot(where[low:high], jnp.concatenate([planes[near - 1], planes[near]], axis=0))
        else:
            compact = packed[low:high].astype(F32)
        if index == 1:
            compact, kept[0] = lax.optimization_barrier((compact, kept[0]))
        if index >= 2:
            compact, relayed[index - 2] = lax.optimization_barrier((compact, relayed[index - 2]))
            spread.append(relay(relayed[index - 2]))
        if index >= 3:
            compact, spread[index - 3] = lax.optimization_barrier((compact, spread[index - 3]))
        scale, main_in = scaled(compact)
        gate = dot(main_in, gate_w) + scale * pad_gate
        upward = dot(main_in, up_w) + scale * pad_up
        hidden = (jax.nn.silu(gate) * upward).astype(BF16)
        worked.append(compact)
        kept.append(hidden)
        relayed.append(lax.ppermute(hidden, "seq", [(0, 2)]))
    sums, relayed[-2] = lax.optimization_barrier((sums, relayed[-2]))
    from_both = exchange_sums(sums)
    spread.append(relay(relayed[-2]))
    spread.append(relay(relayed[-1]))
    from_both, spread[-1] = lax.optimization_barrier((from_both, spread[-1]))
    span_grad = route_sums(sums, from_both)

    at_owner = []
    pad_part = lax.dynamic_slice_in_dim(pad_vector, jnp.maximum(seq - 1, 0) * depth, depth, 0)
    for compact, hidden, at_two, (at_one, at_three) in zip(worked, kept, relayed, spread, strict=True):
        partial = dot_t(pick(seq, [hidden, at_one, at_two, at_three]), down_t)
        residual = jnp.where(seq == 0, compact, pad_part[None, :])
        at_owner.append(partial + jnp.where(member == 0, residual, 0.0))
    at_owner = jnp.concatenate(at_owner, axis=0).reshape(n_seq, n_member, share, depth)

    summed = [sum_members(at_owner[:3].transpose(1, 0, 2, 3).reshape(n_member, 3 * share, depth)).astype(BF16)]
    summed = summed[0].reshape(3, share, depth)
    last = sum_members(at_owner[3]).astype(BF16)
    ready = jnp.concatenate([summed, last[None]], axis=0)
    arrived = [pick(seq, [ready[i] for i in range(n_seq)])]
    for turn in range(1, n_seq):
        sent = pick(seq, [ready[(i + turn) % n_seq] for i in range(n_seq)])
        arrived.append(lax.ppermute(sent, "seq", [(i, (i + turn) % n_seq) for i in range(n_seq)]))
    parts = [pick(seq, [arrived[(s - i) % n_seq] for s in range(n_seq)]) for i in range(n_seq)]
    return (jnp.concatenate(parts, axis=1), span_grad)


def solution(mesh):
    spread = P(("groups", "seq", "mp", "rep"), None)
    weight = P("seq", ("mp", "rep"))
    placed = (spread, spread, P("groups"), P(), P(), P(), P(), P(), weight, weight, weight)
    return jax.shard_map(
        local, mesh=mesh, in_specs=placed, out_specs=(spread, spread), check_vma=False
    )
```

```python
import functools

import jax
import jax.numpy as jnp
from jax import lax
from jax.experimental import pallas as pl
from jax.experimental.pallas import tpu as pltpu
from jax.sharding import PartitionSpec as P

HEAD = 128
WINDOW = 128
CAP = 64
LANE = 24
LANE_ROWS = 32
HALF = 96
GROUP = 32
VMEM = pl.BlockSpec(memory_space=pltpu.VMEM)
ANY = pl.BlockSpec(memory_space=pl.ANY)
HBM = pl.BlockSpec(memory_space=pltpu.HBM)
COST = {'plan': 20000000000, 'tick0': 4000000000, 'tick1': 2000000000, 'tick2': 2000000000, 'tick3': 2000000000, 'tickz': 4000000000, 'early_core': 4000000000}
OPT = {'late_first': 1, 'grads': 1, 'pads': 'rows', 'lag': 1}
CHUNKS = ((0, 3), (3, 7), (7, 12), (12, 16))
PART = ("seq", "mp", "rep")
MEMBER = ("mp", "rep")
F32 = jnp.float32
BF16 = jnp.bfloat16


def dot(a, b):
    return jnp.dot(a, b, preferred_element_type=F32)


def dot_t(a, b):
    return lax.dot_general(a, b, (((1,), (1,)), ((), ())), preferred_element_type=F32)


def is_direct():
    return lax.axis_size("seq") == 4 and lax.axis_size("mp") == 2 and lax.axis_size("rep") == 2


def swap(value, axis):
    return lax.ppermute(value, axis, [(0, 1), (1, 0)])


def kernel_call(kernel, out_shape, *operands, name, after=(), streamed=0, scratch=()):
    count = len(operands)
    body = lambda *refs: kernel(*refs[:count], *refs[count + len(after) :])
    return pl.pallas_call(
        body,
        out_shape=out_shape,
        in_specs=[VMEM] * (count - streamed) + [HBM] * streamed + [ANY] * len(after),
        out_specs=jax.tree.map(lambda _: VMEM, out_shape),
        scratch_shapes=scratch,
        compiler_params=pltpu.CompilerParams(vmem_limit_bytes=24 << 20),
        cost_estimate=pl.CostEstimate(flops=COST.get(name, 0), bytes_accessed=0, transcendentals=0),
        name=name,
    )(*operands, *after)


def tick(name, *after):
    if name not in COST:
        return after[-1]

    def kernel(out_ref):
        out_ref[...] = jnp.zeros_like(out_ref)

    return kernel_call(kernel, array(8, 128, F32), name=name, after=after)


def tie(values, token):
    return lax.optimization_barrier((values, token))


def array(rows, columns, dtype):
    return jax.ShapeDtypeStruct((rows, columns), dtype)


def rms_scale(values, gain):
    return values * lax.rsqrt(jnp.mean(values * values, axis=-1, keepdims=True) + 1e-05) * gain


def encode(x, halo, begin, sel, q_at, enc_gain, w_qkv, w_out):
    length, width = x.shape
    heads = width // HEAD
    both = jnp.concatenate([halo, x], axis=0)
    normed = rms_scale(both.astype(F32), enc_gain).astype(BF16)
    picked = dot(sel, normed[length:]).astype(BF16)
    queries = dot(picked, w_qkv[:, :width]).astype(BF16)
    keyval = dot(normed, w_qkv[:, width:]).astype(BF16)
    k_at = jnp.arange(2 * length, dtype=jnp.int32) - length
    allowed = (
        (k_at[None, :] <= q_at[:, None])
        & (k_at[None, :] > q_at[:, None] - WINDOW)
        & (k_at[None, :] + begin >= 0)
    )
    q_heads = queries.reshape(CAP, heads, HEAD)
    k_heads = keyval[:, :width].reshape(2 * length, heads, HEAD)
    v_heads = keyval[:, width:].reshape(2 * length, heads, HEAD)
    scores = jnp.einsum("qhd,khd->hqk", q_heads, k_heads, preferred_element_type=F32)
    scores = jnp.where(allowed[None], scores / jnp.sqrt(F32(HEAD)), F32(-1e30))
    probs = jax.nn.softmax(scores, axis=-1).astype(BF16)
    mixed = jnp.einsum("hqk,khd->qhd", probs, v_heads, preferred_element_type=F32)
    attended = mixed.reshape(CAP, width).astype(BF16)
    return (dot(sel, x) + dot(attended, w_out)).astype(BF16)


def sum_of_spans(cotangent, span_index):
    n_member = lax.axis_size(MEMBER)
    n_seq = lax.axis_size("seq")
    owner = lax.axis_index("seq")
    length, width = cotangent.shape
    span_own = 32 * n_member
    lowest, highest = span_index[0], span_index[length - 1]
    slot_ids = jnp.arange(CAP, dtype=jnp.int32)
    onehot = (span_index[None, :] - lowest == slot_ids[:, None]).astype(BF16)
    pieces = dot(onehot, cotangent).astype(BF16)
    span_ids = lowest + slot_ids
    valid = (span_ids <= highest)[None, :]
    lane_ids = jnp.arange(LANE, dtype=jnp.int32)
    row_ids = jnp.arange(span_own, dtype=jnp.int32)

    def choose(targets):
        return dot(((targets[:, None] == span_ids[None, :]) & valid).astype(BF16), pieces)

    to_before = choose(owner * span_own - LANE + lane_ids).astype(BF16)
    to_after = choose((owner + 1) * span_own + lane_ids).astype(BF16)
    up = [(i, i + 1) for i in range(n_seq - 1)]
    down = [(i + 1, i) for i in range(n_seq - 1)]
    from_before = lax.ppermute(to_after, "seq", up).astype(F32)
    from_after = lax.ppermute(to_before, "seq", down).astype(F32)
    block = choose(owner * span_own + row_ids)
    block = jnp.concatenate(
        [block[:LANE] + from_before, block[LANE:-LANE], block[-LANE:] + from_after], axis=0
    )
    sent = block.astype(BF16).reshape(n_member, span_own // n_member, width)
    got = lax.all_to_all(sent, MEMBER, 0, 0, tiled=True)
    return jnp.sum(got.astype(F32), axis=0).astype(BF16)


def relay(value):
    return lax.ppermute(value, "seq", [(2, 1)]), lax.ppermute(value, "seq", [(2, 3)])


def lanes_kernel(member_ref, cotangent_ref, own_ref, before_ref, after_ref):
    own = own_ref.shape[0]
    sums = dot(member_ref[...], cotangent_ref[...]).astype(BF16)
    own_ref[...] = sums[:own]
    before_ref[...] = sums[own : own + LANE_ROWS]
    after_ref[...] = sums[own + LANE_ROWS :]


def pad_kernel(pad_ref, gain_ref, gate_ref, up_ref, out_ref):
    seq = lax.axis_index("seq")
    depth = gate_ref.shape[0]
    pad = pad_ref[:, pl.ds(pl.multiple_of(jnp.maximum(seq - 1, 0) * depth, depth), depth)]
    gain = gain_ref[:, pl.ds(pl.multiple_of(seq * depth, depth), depth)]
    high, low = split_high_low(jnp.broadcast_to(pad * gain, (8, depth)))
    both = jnp.concatenate([high, low], axis=0)
    for at, weight_ref in enumerate((gate_ref, up_ref)):
        terms = dot(both, weight_ref[...])
        out_ref[at : at + 1] = jnp.where(seq == 0, 0.0, terms[:1] + terms[8:9])


def plan_kernel(starts_ref, sel_ref, bias_ref, pack_ref, place_ref, member_ref):
    owner, core = lax.axis_index("seq"), lax.axis_index("rep")
    device = owner * 4 + lax.axis_index("mp") * 2 + core
    n_span = starts_ref.shape[1]
    length = sel_ref.shape[1]
    begin = device * length
    row = starts_ref[...]
    column = jnp.transpose(jnp.broadcast_to(row, (length, n_span)))
    here = begin + lax.broadcasted_iota(jnp.int32, (n_span, length), 1)
    earlier = jnp.sum(jnp.where(column < here, 1.0, 0.0), axis=0, keepdims=True).astype(jnp.int32)
    start = jnp.sum(jnp.where(column == here, 1.0, 0.0), axis=0, keepdims=True).astype(jnp.int32)
    slot = lax.broadcasted_iota(jnp.int32, (CAP, length), 0)
    picked = (earlier - earlier[:, :1] == slot) & (start > 0)
    picked = jnp.where(picked, 1.0, 0.0)
    sel_ref[...] = picked.astype(BF16)
    place_in = lax.broadcasted_iota(jnp.int32, (CAP, length), 1).astype(F32)
    q_at = jnp.sum(picked * place_in, axis=1, keepdims=True).astype(jnp.int32)
    k_at = lax.broadcasted_iota(jnp.int32, (CAP, 2 * length), 1) - length
    allowed = (k_at <= q_at) & (k_at > q_at - WINDOW) & (k_at + begin >= 0)
    bias_ref[...] = jnp.where(allowed, 0.0, -1e30)

    span_index = earlier + start - 1
    n_row = member_ref.shape[0]
    own = n_row - 2 * LANE_ROWS
    at = lax.broadcasted_iota(jnp.int32, (n_row, length), 0)
    target = jnp.where(
        at < own, owner * own + at, jnp.where(at < own + LANE_ROWS, owner * own - LANE_ROWS - own, owner * own - LANE_ROWS) + at
    )
    member_ref[...] = jnp.where(span_index == target, 1.0, 0.0).astype(BF16)

    block = owner * 4 + lax.broadcasted_iota(jnp.int32, (n_span, 4 * CAP), 1) // CAP
    first = jnp.sum(jnp.where(column[:, :1] < block * length, 1.0, 0.0), axis=0, keepdims=True).astype(jnp.int32)
    next_first = jnp.sum(jnp.where(column[:, :1] < block * length + length, 1.0, 0.0), axis=0, keepdims=True).astype(jnp.int32)
    lane = lax.broadcasted_iota(jnp.int32, (2 * HALF, 4 * CAP), 1) % CAP
    held = lax.broadcasted_iota(jnp.int32, (2 * HALF, 4 * CAP), 0) + first[:, :1]
    pack_ref[...] = jnp.where((first + lane == held) & (held < next_first), 1.0, 0.0).astype(BF16)

    around = column[:, :1] // (4 * length)
    before = jnp.sum(jnp.where(row < around * (4 * length), 1.0, 0.0), axis=1, keepdims=True).astype(jnp.int32)
    span = lax.broadcasted_iota(jnp.int32, (n_span, 1), 0)
    near = jnp.minimum((span // 32 + 1) // 4, 3)
    lies = span - before
    side = jnp.where(lies >= HALF, 1, 0)
    lies = lies - side * HALF + (side ^ core) * HALF + (around - near + 1) * (2 * HALF)
    lanes = lax.broadcasted_iota(jnp.int32, place_ref.shape, 1)
    place_ref[...] = jnp.where(lanes == lies, 1.0, 0.0).astype(BF16)


def plan(boundaries, length, span_own):
    n_span = boundaries.shape[0]
    return kernel_call(
        plan_kernel,
        (
            array(CAP, length, BF16),
            array(CAP, 2 * length, F32),
            array(2 * HALF, 4 * CAP, BF16),
            array(n_span, 4 * HALF, BF16),
            array(span_own + 2 * LANE_ROWS, length, BF16),
        ),
        boundaries.reshape(1, n_span),
        name="plan",
    )


def encode_kernel(x_ref, halo_ref, sel_ref, bias_ref, gain_ref, qkv_ref, o_ref, out_ref):
    width = x_ref.shape[1]
    wide = 2 * HEAD
    gain = gain_ref[...]
    sel = sel_ref[...]
    bias = bias_ref[...]
    normed = rms_scale(x_ref[...].astype(F32), gain).astype(BF16)
    picked = dot(sel, normed).astype(BF16)
    normed = jnp.concatenate([rms_scale(halo_ref[...].astype(F32), gain).astype(BF16), normed], axis=0)
    mixed = []
    for at in range(0, width, wide):
        queries = dot(picked, qkv_ref[:, at : at + wide]).astype(BF16)
        keys = dot(normed, qkv_ref[:, width + at : width + at + wide]).astype(BF16)
        values = dot(normed, qkv_ref[:, 2 * width + at : 2 * width + at + wide]).astype(BF16)
        for head in range(0, wide, HEAD):
            part = slice(head, head + HEAD)
            scores = dot_t(queries[:, part], keys[:, part]) * (HEAD**-0.5) + bias
            probs = jnp.exp(scores - jnp.max(scores, axis=1, keepdims=True))
            probs = (probs / jnp.sum(probs, axis=1, keepdims=True)).astype(BF16)
            mixed.append(dot(probs, values[:, part]).astype(BF16))
    total = dot(sel, x_ref[...]) + dot(jnp.concatenate(mixed, axis=1), o_ref[...])
    out_ref[...] = total.astype(BF16)


def pair_kernel(rows_ref, came_ref, out_ref):
    chip = lax.axis_index("mp")
    out_ref[:CAP] = jnp.where(chip == 0, rows_ref[...], came_ref[...])
    out_ref[CAP:] = jnp.where(chip == 0, came_ref[...], rows_ref[...])


def pack_kernel(pack_ref, pair_ref, came_ref, mine_ref, other_ref):
    core = lax.axis_index("rep")
    even = jnp.where(core == 0, pair_ref[...], came_ref[...])
    odd = jnp.where(core == 0, came_ref[...], pair_ref[...])
    blocks = [even[:CAP], odd[:CAP], even[CAP:], odd[CAP:]]
    packed = dot(pack_ref[...], jnp.concatenate(blocks, axis=0)).astype(BF16)
    mine_ref[...] = jnp.where(core == 0, packed[:HALF], packed[HALF:])
    other_ref[...] = jnp.where(core == 0, packed[HALF:], packed[:HALF])


def near_of(group):
    return min((group + 1) // 4, 3)


def hidden_kernel(low, high, place_ref, *refs):
    *half_refs, pad_ref, gain_ref, gate_ref, up_ref, term1_ref, term2_ref, term3_ref, hidden_ref, row_ref = refs
    width = row_ref.shape[1]
    base = max(near_of(low) - 1, 0)
    row = []
    while low < high:
        near = near_of(low)
        end = min(high, 4 * near + 3) if near < 3 else high
        total = 0.0
        for seq in (near - 1, near):
            for side in range(2 if seq >= 0 else 0):
                lanes = ((seq - near + 1) * 2 + side) * HALF
                place = place_ref[low * GROUP : end * GROUP, lanes : lanes + HALF]
                total += dot(place, half_refs[(seq - base) * 2 + side][...])
        row.append(total)
        low = end
    row = jnp.concatenate(row, axis=0)
    pad = pad_ref[...]
    total = jnp.sum(row * row, axis=1, keepdims=True) + jnp.sum(pad * pad)
    scale = lax.rsqrt(total / (width + pad.shape[1]) + 1e-05)
    main_in = (row * scale * gain_ref[:, :width]).astype(BF16)
    terms = term1_ref[...] + term2_ref[...] + term3_ref[...]
    gate = dot(main_in, gate_ref[...]) + scale * terms[:1]
    upward = dot(main_in, up_ref[...]) + scale * terms[1:2]
    hidden_ref[...] = (gate / (1.0 + jnp.exp(-gate)) * upward).astype(BF16)
    row_ref[...] = row.astype(BF16)


def hidden_at_zero(*args):
    pl.when(lax.axis_index("seq") == 0)(lambda: hidden_kernel(*args))


def down_kernel(zero_ref, one_ref, two_ref, three_ref, down_ref, row_ref, pad_ref, out_ref):
    seq = lax.axis_index("seq")
    depth = down_ref.shape[0]
    low = jnp.where(seq == 0, zero_ref[...], one_ref[...])
    high = jnp.where(seq == 2, two_ref[...], three_ref[...])
    partial = dot_t(jnp.where(seq < 2, low, high), down_ref[...])
    pad = pad_ref[:, pl.ds(pl.multiple_of(jnp.maximum(seq - 1, 0) * depth, depth), depth)]
    wide = jnp.where(seq == 0, row_ref[...].astype(F32), pad)
    first = (lax.axis_index("mp") == 0) & (lax.axis_index("rep") == 0)
    out_ref[...] = partial + jnp.where(first, wide, 0.0)


def groups_of(refs):
    return [ref.at[at : at + GROUP] for ref in refs for at in range(0, ref.shape[0], GROUP)]


def core_step_kernel(count, *refs):
    core = lax.axis_index("rep")
    groups = groups_of(refs[:count])
    outs = groups_of(refs[count:])
    for at, out in enumerate(outs):
        out[...] = jnp.where(core == 0, groups[2 * at + 1][...], groups[2 * at][...]).astype(BF16)


def chip_step_kernel(count, *refs):
    *came_refs, own_ref, other_ref = refs[count:]
    core, chip = lax.axis_index("rep"), lax.axis_index("mp")
    groups = groups_of(refs[:count])
    came = groups_of(came_refs)
    for at in range(len(groups) // 4):
        first, second = (
            jnp.where(core == 0, groups[4 * at + 2 * i][...], groups[4 * at + 2 * i + 1][...]).astype(F32)
            + came[2 * at + i][...].astype(F32)
            for i in range(2)
        )
        rows = slice(at * GROUP, (at + 1) * GROUP)
        own_ref[rows] = jnp.where(chip == 0, first, second)
        other_ref[rows] = jnp.where(chip == 0, second, first).astype(BF16)


def add_kernel(own_ref, came_ref, *out_refs):
    for at, out_ref in enumerate(out_refs):
        rows = slice(at * GROUP, (at + 1) * GROUP)
        out_ref[...] = (own_ref[rows] + came_ref[rows].astype(F32)).astype(BF16)


def sums_kernel(sums_ref, before_ref, after_ref, out_ref):
    own = out_ref.shape[0]
    out_ref[...] = sums_ref[:own]
    out_ref[:LANE_ROWS] = (sums_ref[:LANE_ROWS].astype(F32) + before_ref[...].astype(F32)).astype(BF16)
    last = slice(own - LANE_ROWS, own)
    out_ref[last] = (sums_ref[last].astype(F32) + after_ref[...].astype(F32)).astype(BF16)


def turn_kernel(own_ref, came_ref, *refs):
    early_refs, out_refs = refs[:3], refs[3:]
    seq = lax.axis_index("seq")
    late = (own_ref[...] + came_ref[...].astype(F32)).astype(BF16)
    groups = [ref[...] for ref in early_refs] + [late]
    for turn, out_ref in enumerate(out_refs):
        owner = (seq + turn) % 4
        value = groups[3]
        for at in range(3):
            value = jnp.where(owner == at, groups[at], value)
        out_ref[...] = value


def join_kernel(*refs):
    *in_refs, out_ref = refs
    seq = lax.axis_index("seq")
    depth = in_refs[0].shape[1]
    for maker in range(4):
        turn = (seq - maker + 4) % 4
        value = in_refs[3][...]
        for at in range(3):
            value = jnp.where(turn == at, in_refs[at][...], value)
        out_ref[:, maker * depth : (maker + 1) * depth] = value


def split_high_low(values):
    high = values.astype(BF16)
    return high, (values - high.astype(F32)).astype(BF16)


def block_first(boundaries, blocks, length):
    edges = jnp.stack([blocks, blocks + 1]) * length
    return jnp.sum((boundaries[:, None, None] < edges[None]).astype(jnp.int32), axis=0)


def place(first, span_ids):
    slots = jnp.arange(CAP, dtype=jnp.int32)
    held = first[0][:, None] + slots[None, :]
    held = jnp.where(held < first[1][:, None], held, -1).reshape(-1)
    return (span_ids[:, None] == held[None, :]).astype(BF16)


def local(
    byte_states,
    cotangent,
    boundaries,
    enc_gain,
    w_qkv,
    w_out,
    pad_vector,
    main_gain,
    gate_w,
    up_w,
    down_t,
):
    n_member = lax.axis_size(MEMBER)
    n_seq = lax.axis_size("seq")
    n_dev = n_seq * n_member
    seq = lax.axis_index("seq")
    device = lax.axis_index(PART)
    length, width = byte_states.shape
    depth, columns = gate_w.shape
    main_width = depth * n_seq
    n_span = boundaries.shape[0]
    share = n_span // n_dev
    begin = device * length

    shift = [(i, i + 1) for i in range(n_dev - 1)]
    halo = lax.ppermute(byte_states, PART, shift)

    direct = is_direct() and depth == width
    if direct:
        pad_row, gain_row = pad_vector.reshape(1, -1), main_gain.reshape(1, -1)
        sel, bias, pack, where, member_of = plan(boundaries, length, n_member * share)
        pad_terms = kernel_call(
            pad_kernel, array(2, columns, F32), pad_row, gain_row, gate_w, up_w, name="pad_terms", after=(sel,)
        )
        rows = kernel_call(
            encode_kernel,
            array(CAP, width, BF16),
            byte_states,
            halo,
            sel,
            bias,
            enc_gain.reshape(1, width),
            w_qkv,
            w_out,
            name="encode",
            after=(pad_terms,) if OPT.get("pads_first", 1) else (),
        )
    else:
        wide_gain = main_gain[width:]
        pad_in = jnp.concatenate([jnp.zeros((width,), F32), pad_vector * wide_gain])
        pad_here = lax.dynamic_slice_in_dim(pad_in, seq * depth, depth, 0)
        pad_rows = jnp.stack(split_high_low(pad_here) * 4)
        pad_terms = jnp.concatenate([dot(pad_rows, gate_w), dot(pad_rows, up_w)], axis=1)
        pad_terms = pad_terms[:1] + pad_terms[1:2]

        places = jnp.arange(length, dtype=jnp.int32)
        earlier = jnp.sum((boundaries[:, None] < begin + places[None, :]).astype(jnp.int32), axis=0)
        starts = jnp.sum((boundaries[:, None] == begin + places[None, :]).astype(jnp.int32), axis=0)
        slot_ids = jnp.arange(CAP, dtype=jnp.int32)
        picks = (earlier - earlier[0] == slot_ids[:, None]) & (starts > 0)
        q_at = jnp.sum(jnp.where(picks, places[None, :], 0), axis=1)
        sel = picks.astype(BF16)
        span_grad = sum_of_spans(cotangent, earlier + starts - 1)
        rows = encode(byte_states, halo, begin, sel, q_at, enc_gain, w_qkv, w_out)

    gain_rows = main_gain[:width]
    pad_square = jnp.sum(pad_vector * pad_vector)

    def scaled(compact):
        squares = jnp.sum(compact * compact, axis=1, keepdims=True) + pad_square
        scale = lax.rsqrt(squares / main_width + 1e-05)
        return scale, (compact * scale * gain_rows).astype(BF16)

    if not direct:
        gathered = lax.all_gather(rows, PART, axis=0, tiled=True)
        order = jnp.arange(n_span, dtype=jnp.int32).reshape(n_seq, n_member, share)
        order = order.transpose(1, 0, 2).reshape(-1)
        first = block_first(boundaries, jnp.arange(n_dev, dtype=jnp.int32), length)
        compact = dot(place(first, order), gathered)
        scale, main_in = scaled(compact)
        padded = jnp.pad(main_in, ((0, 0), (0, main_width - width)))
        here = lax.dynamic_slice_in_dim(padded, seq * depth, depth, 1)
        gate = dot(here, gate_w) + scale * pad_terms[:, :columns]
        upward = dot(here, up_w) + scale * pad_terms[:, columns:]
        gate, upward = lax.psum((gate, upward), "seq")
        hidden = (jax.nn.silu(gate) * upward).astype(BF16)
        partial = dot_t(hidden, down_t).astype(BF16).reshape(n_member, n_seq * share, depth)
        got = lax.all_to_all(partial, MEMBER, 0, 0, tiled=True)
        summed = jnp.sum(got.astype(F32), axis=0)
        member = lax.axis_index(MEMBER)
        mine = lax.dynamic_slice_in_dim(compact, member * n_seq * share, n_seq * share, 0)
        wide = jnp.concatenate(
            [mine, jnp.broadcast_to(pad_vector, (n_seq * share, main_width - width))], axis=1
        )
        residual = lax.dynamic_slice_in_dim(wide, seq * depth, depth, 1)
        done = (summed + residual).astype(BF16).reshape(n_seq, share, depth)
        spread = lax.all_to_all(done, "seq", 0, 0, tiled=True)
        main_out = spread.transpose(1, 0, 2).reshape(share, main_width)
        return (main_out, span_grad)

    from_chip = swap(rows, "mp")
    if OPT.get("pads") == "rows":
        pad_terms, rows = tie(pad_terms, rows)
    terms = [lax.ppermute(pad_terms, "seq", [(j, 0)]) for j in range(1, n_seq)]
    pair = kernel_call(pair_kernel, array(2 * CAP, width, BF16), rows, from_chip, name="pair")
    mine, other = kernel_call(pack_kernel, (array(HALF, width, BF16),) * 2, pack, pair, swap(pair, "rep"), name="pack")
    planes = [(mine, other)]
    came = [lax.ppermute(mine, "seq", [(j, 0)]) for j in range(1, n_seq)]

    def over_cores(values, name):
        quarters = sum(value.shape[0] for value in values) // GROUP // 4
        sent = kernel_call(
            functools.partial(core_step_kernel, len(values)),
            (array(2 * GROUP, depth, BF16),) * quarters,
            *values,
            name=name + "_core",
        )
        return kernel_call(
            functools.partial(chip_step_kernel, len(values)),
            (array(quarters * GROUP, depth, F32), array(quarters * GROUP, depth, BF16)),
            *values,
            *(swap(value, "rep") for value in sent),
            name=name + "_chip",
        )

    hiddens, row_parts, relayed, spread, parts = [], [], [], [], []

    def make_hidden(index, *after):
        if OPT.get("lean") and index:
            after = after[-1:]
        low, high = CHUNKS[index]
        halves = [half for plane in planes[max(near_of(low) - 1, 0) : near_of(high - 1) + 1] for half in plane]
        count = (high - low) * share
        hidden, row = kernel_call(
            functools.partial(hidden_at_zero, low, high),
            (array(count, columns, BF16), array(count, width, BF16)),
            where,
            *halves,
            pad_row,
            gain_row,
            gate_w,
            up_w,
            *terms,
            name=f"hidden{index}",
            after=after,
        )
        hiddens.append(hidden)
        row_parts.append(row)
        relayed.append(lax.ppermute(hidden, "seq", [(0, 2)]))

    def make_part(index, *after):
        at_one, at_three = spread[index]
        count = row_parts[index].shape[0]
        parts.append(
            kernel_call(
                down_kernel,
                array(count, depth, F32),
                hiddens[index],
                at_one,
                relayed[index],
                at_three,
                down_t,
                row_parts[index],
                pad_row,
                name=f"down{index}",
                after=after,
            )
        )

    def take(index, token):
        arrived, token = tie(came[index], token)
        planes.append((arrived, swap(arrived, "rep")))
        return token

    def pass_on(index, token):
        relayed[index], token = tie(relayed[index], token)
        spread.append(relay(relayed[index]))
        return relayed[index], token

    n_chunk = len(CHUNKS)
    early = sum(high <= 12 for _, high in CHUNKS)
    n_chunk = len(CHUNKS)
    early = sum(high <= 12 for _, high in CHUNKS)
    make_hidden(0)
    token = take(2, take(1, take(0, tick("tickz", hiddens[0]))))
    ahead = OPT.get("ahead", n_chunk - 1)
    for index in range(1, ahead + 1):
        make_hidden(index, token)
        token = hiddens[index]
    grads = OPT.get("grads", 2)
    for index in range(n_chunk):
        after = pass_on(index, tick(f"tickx{index}", token))
        token = after[1]
        if ahead + 1 + index < n_chunk:
            make_hidden(ahead + 1 + index, *after)
            token = hiddens[-1]
        token = tick(f"tick{index}", token)
        ready_part = index - OPT.get("lag", 1)
        if ready_part >= 0:
            make_part(ready_part, token, *after[:1])
            token = parts[-1]
        if index == grads:
            sums, to_before, to_after = kernel_call(
                lanes_kernel,
                (array(n_member * share, width, BF16), array(LANE_ROWS, width, BF16), array(LANE_ROWS, width, BF16)),
                member_of,
                cotangent,
                name="lanes",
                after=(token,),
            )
            up = [(i, i + 1) for i in range(n_seq - 1)]
            down = [(i + 1, i) for i in range(n_seq - 1)]
            from_both = lax.ppermute(to_after, "seq", up), lax.ppermute(to_before, "seq", down)
            token = sums
    while len(parts) < early:
        make_part(len(parts), token)
        token = parts[-1]
    block = kernel_call(
        sums_kernel, array(n_member * share, width, BF16), sums, *from_both, name="span_sums", after=(token,)
    )
    values = [*parts[:early], block]
    own, sent = over_cores(values, "early")
    from_mp = swap(sent, "mp")
    token = sent
    while len(parts) < n_chunk - 1:
        make_part(len(parts), token)
        token = parts[-1]
    late_first = OPT.get("late_first", 0)

    def add_early(*after):
        *ready, span_grad = kernel_call(
            add_kernel, (array(GROUP, depth, BF16),) * 4, own, from_mp, name="early_add", after=after
        )
        return ready, span_grad

    if not late_first:
        ready, span_grad = add_early(token)
        token = ready[0]
    if len(parts) < n_chunk:
        make_part(n_chunk - 1, tick("tick6", token))
    late_own, late_sent = over_cores(parts[early:], "late")
    if late_first:
        ready, span_grad = add_early(late_sent)
    own, sent = late_own, late_sent

    turned = kernel_call(
        turn_kernel, (array(GROUP, depth, BF16),) * n_seq, own, swap(sent, "mp"), *ready, name="turn"
    )
    arrived = [turned[0]]
    for turn in range(1, n_seq):
        pairs = [(i, (i + turn) % n_seq) for i in range(n_seq)]
        arrived.append(lax.ppermute(turned[turn], "seq", pairs))
    main_out = kernel_call(join_kernel, array(share, main_width, BF16), *arrived, name="join")
    return (main_out, span_grad)


def solution(mesh):
    spread = P(("groups", "seq", "mp", "rep"), None)
    weight = P("seq", ("mp", "rep"))
    placed = (spread, spread, P("groups"), P(), P(), P(), P(), P(), weight, weight, weight)
    return jax.shard_map(
        local, mesh=mesh, in_specs=placed, out_specs=(spread, spread), check_vma=False
    )
```

```python
import functools

import jax
import jax.numpy as jnp
from jax import lax
from jax.experimental import pallas as pl
from jax.experimental.pallas import tpu as pltpu
from jax.sharding import PartitionSpec as P

HEAD = 128
WINDOW = 128
CAP = 64
LANE = 24
LANE_ROWS = 32
GROUP = 32
VMEM = pl.BlockSpec(memory_space=pltpu.VMEM)
ANY = pl.BlockSpec(memory_space=pl.ANY)
HBM = pl.BlockSpec(memory_space=pltpu.HBM)
COST = {
    "plan": 20_000_000_000,
    "tick0": 4_000_000_000,
    "tick1": 2_000_000_000,
    "tick2": 2_000_000_000,
    "tick3": 2_000_000_000,
    "tickz": 2_000_000_000,
    "early_core": 4_000_000_000,
    "encode": 20_000_000_000,
    "hidden0": 2_000_000_000,
}
CHUNKS = ((0, 3), (3, 7), (7, 12), (12, 16))
EARLY = 3
PART = ("seq", "mp", "rep")
MEMBER = ("mp", "rep")
F32 = jnp.float32
BF16 = jnp.bfloat16


def dot(a, b):
    return jnp.dot(a, b, preferred_element_type=F32)


def dot_t(a, b):
    return lax.dot_general(a, b, (((1,), (1,)), ((), ())), preferred_element_type=F32)


def is_direct():
    return lax.axis_size("seq") == 4 and lax.axis_size("mp") == 2 and lax.axis_size("rep") == 2


def swap(value, axis):
    return lax.ppermute(value, axis, [(0, 1), (1, 0)])


def kernel_call(kernel, out_shape, *operands, name, after=(), streamed=0, scratch=()):
    count = len(operands)
    body = lambda *refs: kernel(*refs[:count], *refs[count + len(after) :])
    return pl.pallas_call(
        body,
        out_shape=out_shape,
        in_specs=[VMEM] * (count - streamed) + [HBM] * streamed + [ANY] * len(after),
        out_specs=jax.tree.map(lambda _: VMEM, out_shape),
        scratch_shapes=scratch,
        compiler_params=pltpu.CompilerParams(vmem_limit_bytes=24 << 20),
        cost_estimate=pl.CostEstimate(flops=COST.get(name, 0), bytes_accessed=0, transcendentals=0),
        name=name,
    )(*operands, *after)


def tick(name, *after):
    def kernel(out_ref):
        out_ref[...] = jnp.zeros_like(out_ref)

    return kernel_call(kernel, array(8, 128, F32), name=name, after=after)


def tie(values, token):
    return lax.optimization_barrier((values, token))


def array(rows, columns, dtype):
    return jax.ShapeDtypeStruct((rows, columns), dtype)


def rms_scale(values, gain):
    return values * lax.rsqrt(jnp.mean(values * values, axis=-1, keepdims=True) + 1e-05) * gain


def encode(x, halo, begin, sel, q_at, enc_gain, w_qkv, w_out):
    length, width = x.shape
    heads = width // HEAD
    both = jnp.concatenate([halo, x], axis=0)
    normed = rms_scale(both.astype(F32), enc_gain).astype(BF16)
    picked = dot(sel, normed[length:]).astype(BF16)
    queries = dot(picked, w_qkv[:, :width]).astype(BF16)
    keyval = dot(normed, w_qkv[:, width:]).astype(BF16)
    k_at = jnp.arange(2 * length, dtype=jnp.int32) - length
    allowed = (
        (k_at[None, :] <= q_at[:, None])
        & (k_at[None, :] > q_at[:, None] - WINDOW)
        & (k_at[None, :] + begin >= 0)
    )
    q_heads = queries.reshape(CAP, heads, HEAD)
    k_heads = keyval[:, :width].reshape(2 * length, heads, HEAD)
    v_heads = keyval[:, width:].reshape(2 * length, heads, HEAD)
    scores = jnp.einsum("qhd,khd->hqk", q_heads, k_heads, preferred_element_type=F32)
    scores = jnp.where(allowed[None], scores / jnp.sqrt(F32(HEAD)), F32(-1e30))
    probs = jax.nn.softmax(scores, axis=-1).astype(BF16)
    mixed = jnp.einsum("hqk,khd->qhd", probs, v_heads, preferred_element_type=F32)
    attended = mixed.reshape(CAP, width).astype(BF16)
    return (dot(sel, x) + dot(attended, w_out)).astype(BF16)


def sum_of_spans(cotangent, span_index):
    n_member = lax.axis_size(MEMBER)
    n_seq = lax.axis_size("seq")
    owner = lax.axis_index("seq")
    length, width = cotangent.shape
    span_own = 32 * n_member
    lowest, highest = span_index[0], span_index[length - 1]
    slot_ids = jnp.arange(CAP, dtype=jnp.int32)
    onehot = (span_index[None, :] - lowest == slot_ids[:, None]).astype(BF16)
    pieces = dot(onehot, cotangent).astype(BF16)
    span_ids = lowest + slot_ids
    valid = (span_ids <= highest)[None, :]
    lane_ids = jnp.arange(LANE, dtype=jnp.int32)
    row_ids = jnp.arange(span_own, dtype=jnp.int32)

    def choose(targets):
        return dot(((targets[:, None] == span_ids[None, :]) & valid).astype(BF16), pieces)

    to_before = choose(owner * span_own - LANE + lane_ids).astype(BF16)
    to_after = choose((owner + 1) * span_own + lane_ids).astype(BF16)
    up = [(i, i + 1) for i in range(n_seq - 1)]
    down = [(i + 1, i) for i in range(n_seq - 1)]
    from_before = lax.ppermute(to_after, "seq", up).astype(F32)
    from_after = lax.ppermute(to_before, "seq", down).astype(F32)
    block = choose(owner * span_own + row_ids)
    block = jnp.concatenate(
        [block[:LANE] + from_before, block[LANE:-LANE], block[-LANE:] + from_after], axis=0
    )
    sent = block.astype(BF16).reshape(n_member, span_own // n_member, width)
    got = lax.all_to_all(sent, MEMBER, 0, 0, tiled=True)
    return jnp.sum(got.astype(F32), axis=0).astype(BF16)


def relay(value):
    return lax.ppermute(value, "seq", [(2, 1)]), lax.ppermute(value, "seq", [(2, 3)])


def lanes_kernel(member_ref, cotangent_ref, own_ref, before_ref, after_ref):
    own = own_ref.shape[0]
    sums = dot(member_ref[...], cotangent_ref[...]).astype(BF16)
    own_ref[...] = sums[:own]
    before_ref[...] = sums[own : own + LANE_ROWS]
    after_ref[...] = sums[own + LANE_ROWS :]


def pad_kernel(pad_ref, gain_ref, gate_ref, up_ref, out_ref):
    seq = lax.axis_index("seq")
    depth = gate_ref.shape[0]
    pad = pad_ref[:, pl.ds(pl.multiple_of(jnp.maximum(seq - 1, 0) * depth, depth), depth)]
    gain = gain_ref[:, pl.ds(pl.multiple_of(seq * depth, depth), depth)]
    high, low = split_high_low(jnp.broadcast_to(pad * gain, (8, depth)))
    both = jnp.concatenate([high, low], axis=0)
    for at, weight_ref in enumerate((gate_ref, up_ref)):
        terms = dot(both, weight_ref[...])
        out_ref[at : at + 1] = jnp.where(seq == 0, 0.0, terms[:1] + terms[8:9])


def plan_kernel(starts_ref, sel_ref, bias_ref, place_ref, member_ref):
    owner, core = lax.axis_index("seq"), lax.axis_index("rep")
    here_member = lax.axis_index("mp") * 2 + core
    device = owner * 4 + here_member
    n_span = starts_ref.shape[1]
    length = sel_ref.shape[1]
    begin = device * length
    row = starts_ref[...]
    column = jnp.transpose(jnp.broadcast_to(row, (length, n_span)))
    here = begin + lax.broadcasted_iota(jnp.int32, (n_span, length), 1)
    earlier = jnp.sum(jnp.where(column < here, 1.0, 0.0), axis=0, keepdims=True).astype(jnp.int32)
    start = jnp.sum(jnp.where(column == here, 1.0, 0.0), axis=0, keepdims=True).astype(jnp.int32)
    slot = lax.broadcasted_iota(jnp.int32, (CAP, length), 0)
    picked = (earlier - earlier[:, :1] == slot) & (start > 0)
    picked = jnp.where(picked, 1.0, 0.0)
    sel_ref[...] = picked.astype(BF16)
    place_in = lax.broadcasted_iota(jnp.int32, (CAP, length), 1).astype(F32)
    q_at = jnp.sum(picked * place_in, axis=1, keepdims=True).astype(jnp.int32)
    k_at = lax.broadcasted_iota(jnp.int32, (CAP, 2 * length), 1) - length
    allowed = (k_at <= q_at) & (k_at > q_at - WINDOW) & (k_at + begin >= 0)
    bias_ref[...] = jnp.where(allowed, 0.0, -1e30)

    span_index = earlier + start - 1
    n_row = member_ref.shape[0]
    own = n_row - 2 * LANE_ROWS
    at = lax.broadcasted_iota(jnp.int32, (n_row, length), 0)
    target = jnp.where(
        at < own, owner * own + at, jnp.where(at < own + LANE_ROWS, owner * own - LANE_ROWS - own, owner * own - LANE_ROWS) + at
    )
    member_ref[...] = jnp.where(span_index == target, 1.0, 0.0).astype(BF16)

    block = column[:, :1] // length
    before = jnp.sum(jnp.where(row < block * length, 1.0, 0.0), axis=1, keepdims=True).astype(jnp.int32)
    span = lax.broadcasted_iota(jnp.int32, (n_span, 1), 0)
    near = jnp.minimum((span // 32 + 1) // 4, 3)
    turned = (block % 4) ^ here_member
    turned = (turned % 2) * 2 + turned // 2
    lies = ((block // 4 - near + 1) * 4 + turned) * CAP + span - before
    lanes = lax.broadcasted_iota(jnp.int32, place_ref.shape, 1)
    place_ref[...] = jnp.where(lanes == lies, 1.0, 0.0).astype(BF16)


def plan(boundaries, length, span_own):
    n_span = boundaries.shape[0]
    return kernel_call(
        plan_kernel,
        (
            array(CAP, length, BF16),
            array(CAP, 2 * length, F32),
            array(n_span, 8 * CAP, BF16),
            array(span_own + 2 * LANE_ROWS, length, BF16),
        ),
        boundaries.reshape(1, n_span),
        name="plan",
    )


def project(normed, qkv_ref, at):
    width = normed.shape[1]
    wide = 2 * HEAD
    keys = dot(normed, qkv_ref[:, width + at : width + at + wide]).astype(BF16)
    values = dot(normed, qkv_ref[:, 2 * width + at : 2 * width + at + wide]).astype(BF16)
    return keys, values


def own_kernel(x_ref, sel_ref, gain_ref, qkv_ref, q_ref, kv_ref):
    width = x_ref.shape[1]
    wide = 2 * HEAD
    normed = rms_scale(x_ref[...].astype(F32), gain_ref[...]).astype(BF16)
    picked = dot(sel_ref[...], normed).astype(BF16)
    for at in range(0, width, wide):
        q_ref[:, at : at + wide] = dot(picked, qkv_ref[:, at : at + wide]).astype(BF16)
        keys, values = project(normed, qkv_ref, at)
        kv_ref[:, at : at + wide] = keys
        kv_ref[:, width + at : width + at + wide] = values


def encode_kernel(x_ref, halo_ref, sel_ref, bias_ref, gain_ref, qkv_ref, o_ref, q_ref, kv_ref, out_ref):
    width = x_ref.shape[1]
    wide = 2 * HEAD
    sel = sel_ref[...]
    bias = bias_ref[...]
    normed = rms_scale(halo_ref[...].astype(F32), gain_ref[...]).astype(BF16)
    mixed = []
    for at in range(0, width, wide):
        queries = q_ref[:, at : at + wide]
        keys, values = project(normed, qkv_ref, at)
        keys = jnp.concatenate([keys, kv_ref[:, at : at + wide]], axis=0)
        values = jnp.concatenate([values, kv_ref[:, width + at : width + at + wide]], axis=0)
        for head in range(0, wide, HEAD):
            part = slice(head, head + HEAD)
            scores = dot_t(queries[:, part], keys[:, part]) * (HEAD**-0.5) + bias
            probs = jnp.exp(scores - jnp.max(scores, axis=1, keepdims=True))
            probs = (probs / jnp.sum(probs, axis=1, keepdims=True)).astype(BF16)
            mixed.append(dot(probs, values[:, part]).astype(BF16))
    total = dot(sel, x_ref[...]) + dot(jnp.concatenate(mixed, axis=1), o_ref[...])
    out_ref[...] = total.astype(BF16)


def terms_kernel(*refs):
    *in_refs, out_ref = refs
    out_ref[...] = sum(ref[...] for ref in in_refs)


def near_of(group):
    return min((group + 1) // 4, 3)


def hidden_kernel(low, high, place_ref, *refs):
    base = max(near_of(low) - 1, 0)
    count = 4 * (near_of(high - 1) - base + 1)
    block_refs, refs = refs[:count], refs[count:]
    pad_ref, gain_ref, gate_ref, up_ref, term_ref, hidden_ref, row_ref = refs
    width = row_ref.shape[1]
    row = []
    while low < high:
        near = near_of(low)
        end = min(high, 4 * near + 3) if near < 3 else high
        total = 0.0
        for seq in range(max(near - 1, 0), near + 1):
            blocks = jnp.concatenate([ref[...] for ref in block_refs[(seq - base) * 4 : (seq - base) * 4 + 4]], axis=0)
            lanes = (seq - near + 1) * 4 * CAP
            total += dot(place_ref[low * GROUP : end * GROUP, lanes : lanes + 4 * CAP], blocks)
        row.append(total)
        low = end
    row = jnp.concatenate(row, axis=0)
    pad = pad_ref[...]
    total = jnp.sum(row * row, axis=1, keepdims=True) + jnp.sum(pad * pad)
    scale = lax.rsqrt(total / (width + pad.shape[1]) + 1e-05)
    main_in = (row * scale * gain_ref[:, :width]).astype(BF16)
    terms = term_ref[...]
    gate = dot(main_in, gate_ref[...]) + scale * terms[:1]
    upward = dot(main_in, up_ref[...]) + scale * terms[1:2]
    hidden_ref[...] = (gate / (1.0 + jnp.exp(-gate)) * upward).astype(BF16)
    row_ref[...] = row.astype(BF16)


def hidden_at_zero(*args):
    pl.when(lax.axis_index("seq") == 0)(lambda: hidden_kernel(*args))


def down_kernel(zero_ref, one_ref, two_ref, three_ref, down_ref, row_ref, pad_ref, out_ref):
    seq = lax.axis_index("seq")
    depth = down_ref.shape[0]
    low = jnp.where(seq == 0, zero_ref[...], one_ref[...])
    high = jnp.where(seq == 2, two_ref[...], three_ref[...])
    partial = dot_t(jnp.where(seq < 2, low, high), down_ref[...])
    pad = pad_ref[:, pl.ds(pl.multiple_of(jnp.maximum(seq - 1, 0) * depth, depth), depth)]
    wide = jnp.where(seq == 0, row_ref[...].astype(F32), pad)
    first = (lax.axis_index("mp") == 0) & (lax.axis_index("rep") == 0)
    out_ref[...] = partial + jnp.where(first, wide, 0.0)


def groups_of(refs):
    return [ref.at[at : at + GROUP] for ref in refs for at in range(0, ref.shape[0], GROUP)]


def core_step_kernel(count, *refs):
    core = lax.axis_index("rep")
    groups = groups_of(refs[:count])
    outs = groups_of(refs[count:])
    for at, out in enumerate(outs):
        out[...] = jnp.where(core == 0, groups[2 * at + 1][...], groups[2 * at][...]).astype(BF16)


def chip_step_kernel(count, *refs):
    *came_refs, own_ref, other_ref = refs[count:]
    core, chip = lax.axis_index("rep"), lax.axis_index("mp")
    groups = groups_of(refs[:count])
    came = groups_of(came_refs)
    for at in range(len(groups) // 4):
        first, second = (
            jnp.where(core == 0, groups[4 * at + 2 * i][...], groups[4 * at + 2 * i + 1][...]).astype(F32)
            + came[2 * at + i][...].astype(F32)
            for i in range(2)
        )
        rows = slice(at * GROUP, (at + 1) * GROUP)
        own_ref[rows] = jnp.where(chip == 0, first, second)
        other_ref[rows] = jnp.where(chip == 0, second, first).astype(BF16)


def add_kernel(own_ref, came_ref, *out_refs):
    for at, out_ref in enumerate(out_refs):
        rows = slice(at * GROUP, (at + 1) * GROUP)
        out_ref[...] = (own_ref[rows] + came_ref[rows].astype(F32)).astype(BF16)


def sums_kernel(sums_ref, before_ref, after_ref, out_ref):
    own = out_ref.shape[0]
    out_ref[...] = sums_ref[:own]
    out_ref[:LANE_ROWS] = (sums_ref[:LANE_ROWS].astype(F32) + before_ref[...].astype(F32)).astype(BF16)
    last = slice(own - LANE_ROWS, own)
    out_ref[last] = (sums_ref[last].astype(F32) + after_ref[...].astype(F32)).astype(BF16)


def turn_kernel(own_ref, came_ref, *refs):
    early_refs, out_refs = refs[:3], refs[3:]
    seq = lax.axis_index("seq")
    late = (own_ref[...] + came_ref[...].astype(F32)).astype(BF16)
    groups = [ref[...] for ref in early_refs] + [late]
    for turn, out_ref in enumerate(out_refs):
        owner = (seq + turn) % 4
        value = groups[3]
        for at in range(3):
            value = jnp.where(owner == at, groups[at], value)
        out_ref[...] = value


def join_kernel(*refs):
    *in_refs, out_ref = refs
    seq = lax.axis_index("seq")
    depth = in_refs[0].shape[1]
    for maker in range(4):
        turn = (seq - maker + 4) % 4
        value = in_refs[3][...]
        for at in range(3):
            value = jnp.where(turn == at, in_refs[at][...], value)
        out_ref[:, maker * depth : (maker + 1) * depth] = value


def split_high_low(values):
    high = values.astype(BF16)
    return high, (values - high.astype(F32)).astype(BF16)


def block_first(boundaries, blocks, length):
    edges = jnp.stack([blocks, blocks + 1]) * length
    return jnp.sum((boundaries[:, None, None] < edges[None]).astype(jnp.int32), axis=0)


def place(first, span_ids):
    slots = jnp.arange(CAP, dtype=jnp.int32)
    held = first[0][:, None] + slots[None, :]
    held = jnp.where(held < first[1][:, None], held, -1).reshape(-1)
    return (span_ids[:, None] == held[None, :]).astype(BF16)


def local(
    byte_states,
    cotangent,
    boundaries,
    enc_gain,
    w_qkv,
    w_out,
    pad_vector,
    main_gain,
    gate_w,
    up_w,
    down_t,
):
    n_member = lax.axis_size(MEMBER)
    n_seq = lax.axis_size("seq")
    n_dev = n_seq * n_member
    seq = lax.axis_index("seq")
    device = lax.axis_index(PART)
    length, width = byte_states.shape
    depth, columns = gate_w.shape
    main_width = depth * n_seq
    n_span = boundaries.shape[0]
    share = n_span // n_dev
    begin = device * length

    shift = [(i, i + 1) for i in range(n_dev - 1)]
    halo = lax.ppermute(byte_states, PART, shift)

    direct = is_direct() and depth == width
    if direct:
        pad_row, gain_row = pad_vector.reshape(1, -1), main_gain.reshape(1, -1)
        sel, bias, where, member_of = plan(boundaries, length, n_member * share)
        pad_terms = kernel_call(
            pad_kernel, array(2, columns, F32), pad_row, gain_row, gate_w, up_w, name="pad_terms", after=(sel,)
        )
        own = kernel_call(
            own_kernel,
            (array(CAP, width, BF16), array(length, 2 * width, BF16)),
            byte_states,
            sel,
            enc_gain.reshape(1, width),
            w_qkv,
            name="own",
            after=(pad_terms,),
        )
        rows = kernel_call(
            encode_kernel,
            array(CAP, width, BF16),
            byte_states,
            halo,
            sel,
            bias,
            enc_gain.reshape(1, width),
            w_qkv,
            w_out,
            *own,
            name="encode",
            after=(pad_terms,),
        )
    else:
        wide_gain = main_gain[width:]
        pad_in = jnp.concatenate([jnp.zeros((width,), F32), pad_vector * wide_gain])
        pad_here = lax.dynamic_slice_in_dim(pad_in, seq * depth, depth, 0)
        pad_rows = jnp.stack(split_high_low(pad_here) * 4)
        pad_terms = jnp.concatenate([dot(pad_rows, gate_w), dot(pad_rows, up_w)], axis=1)
        pad_terms = pad_terms[:1] + pad_terms[1:2]

        places = jnp.arange(length, dtype=jnp.int32)
        earlier = jnp.sum((boundaries[:, None] < begin + places[None, :]).astype(jnp.int32), axis=0)
        starts = jnp.sum((boundaries[:, None] == begin + places[None, :]).astype(jnp.int32), axis=0)
        slot_ids = jnp.arange(CAP, dtype=jnp.int32)
        picks = (earlier - earlier[0] == slot_ids[:, None]) & (starts > 0)
        q_at = jnp.sum(jnp.where(picks, places[None, :], 0), axis=1)
        sel = picks.astype(BF16)
        span_grad = sum_of_spans(cotangent, earlier + starts - 1)
        rows = encode(byte_states, halo, begin, sel, q_at, enc_gain, w_qkv, w_out)

    gain_rows = main_gain[:width]
    pad_square = jnp.sum(pad_vector * pad_vector)

    def scaled(compact):
        squares = jnp.sum(compact * compact, axis=1, keepdims=True) + pad_square
        scale = lax.rsqrt(squares / main_width + 1e-05)
        return scale, (compact * scale * gain_rows).astype(BF16)

    if not direct:
        gathered = lax.all_gather(rows, PART, axis=0, tiled=True)
        order = jnp.arange(n_span, dtype=jnp.int32).reshape(n_seq, n_member, share)
        order = order.transpose(1, 0, 2).reshape(-1)
        first = block_first(boundaries, jnp.arange(n_dev, dtype=jnp.int32), length)
        compact = dot(place(first, order), gathered)
        scale, main_in = scaled(compact)
        padded = jnp.pad(main_in, ((0, 0), (0, main_width - width)))
        here = lax.dynamic_slice_in_dim(padded, seq * depth, depth, 1)
        gate = dot(here, gate_w) + scale * pad_terms[:, :columns]
        upward = dot(here, up_w) + scale * pad_terms[:, columns:]
        gate, upward = lax.psum((gate, upward), "seq")
        hidden = (jax.nn.silu(gate) * upward).astype(BF16)
        partial = dot_t(hidden, down_t).astype(BF16).reshape(n_member, n_seq * share, depth)
        got = lax.all_to_all(partial, MEMBER, 0, 0, tiled=True)
        summed = jnp.sum(got.astype(F32), axis=0)
        member = lax.axis_index(MEMBER)
        mine = lax.dynamic_slice_in_dim(compact, member * n_seq * share, n_seq * share, 0)
        wide = jnp.concatenate(
            [mine, jnp.broadcast_to(pad_vector, (n_seq * share, main_width - width))], axis=1
        )
        residual = lax.dynamic_slice_in_dim(wide, seq * depth, depth, 1)
        done = (summed + residual).astype(BF16).reshape(n_seq, share, depth)
        spread = lax.all_to_all(done, "seq", 0, 0, tiled=True)
        main_out = spread.transpose(1, 0, 2).reshape(share, main_width)
        return (main_out, span_grad)

    terms = [lax.ppermute(pad_terms, "seq", [(j, 0)]) for j in range(n_seq - 1, 0, -1)]
    terms = kernel_call(terms_kernel, array(2, columns, F32), *terms, name="terms", after=(rows,))
    rows, terms = tie(rows, terms)
    def to_members(value):
        from_chip = swap(value, "mp")
        return value, from_chip, swap(value, "rep"), swap(from_chip, "rep")

    came = [lax.ppermute(rows, "seq", [(j, 0)]) for j in range(1, n_seq)]
    across = lax.ppermute(rows, MEMBER, [(j, 3 - j) for j in range(4)])
    planes = [(rows, swap(rows, "mp"), swap(rows, "rep"), across)]

    def over_cores(values, name):
        quarters = sum(value.shape[0] for value in values) // GROUP // 4
        sent = kernel_call(
            functools.partial(core_step_kernel, len(values)),
            (array(2 * GROUP, depth, BF16),) * quarters,
            *values,
            name=name + "_core",
        )
        return kernel_call(
            functools.partial(chip_step_kernel, len(values)),
            (array(quarters * GROUP, depth, F32), array(quarters * GROUP, depth, BF16)),
            *values,
            *(swap(value, "rep") for value in sent),
            name=name + "_chip",
        )

    hiddens, row_parts, relayed, spread, parts = [], [], [], [], []

    def make_hidden(index, *after):
        low, high = CHUNKS[index]
        halves = [block for plane in planes[max(near_of(low) - 1, 0) : near_of(high - 1) + 1] for block in plane]
        count = (high - low) * share
        hidden, row = kernel_call(
            functools.partial(hidden_at_zero, low, high),
            (array(count, columns, BF16), array(count, width, BF16)),
            where,
            *halves,
            pad_row,
            gain_row,
            gate_w,
            up_w,
            terms,
            name=f"hidden{index}",
            after=after,
        )
        hiddens.append(hidden)
        row_parts.append(row)
        relayed.append(lax.ppermute(hidden, "seq", [(0, 2)]))

    def make_part(index, *after):
        at_one, at_three = spread[index]
        count = row_parts[index].shape[0]
        parts.append(
            kernel_call(
                down_kernel,
                array(count, depth, F32),
                hiddens[index],
                at_one,
                relayed[index],
                at_three,
                down_t,
                row_parts[index],
                pad_row,
                name=f"down{index}",
                after=after,
            )
        )

    def pass_on(index, token):
        relayed[index], token = tie(relayed[index], token)
        spread.append(relay(relayed[index]))
        return relayed[index], token

    value, token = tie(came[0], rows)
    planes.append(to_members(value))
    make_hidden(0, token)
    token = tick("tickz", hiddens[0])
    later = []
    for value in came[1:]:
        value, token = tie(value, token)
        later.append((value, swap(value, "mp"), swap(value, "rep")))
    make_hidden(1, token)
    token = hiddens[1]
    for value, from_chip, from_core in later:
        from_chip, token = tie(from_chip, token)
        planes.append((value, from_chip, from_core, swap(from_chip, "rep")))
    make_hidden(2, token)
    make_hidden(3, hiddens[2])
    token = hiddens[3]
    for index in range(len(CHUNKS)):
        arrived, token = pass_on(index, token)
        token = tick(f"tick{index}", token)
        if index:
            make_part(index - 1, token, arrived)
            token = parts[-1]
        if index == 1:
            sums, to_before, to_after = kernel_call(
                lanes_kernel,
                (array(n_member * share, width, BF16),) + (array(LANE_ROWS, width, BF16),) * 2,
                member_of,
                cotangent,
                name="lanes",
                after=(token,),
            )
            up = [(i, i + 1) for i in range(n_seq - 1)]
            down = [(i + 1, i) for i in range(n_seq - 1)]
            from_both = lax.ppermute(to_after, "seq", up), lax.ppermute(to_before, "seq", down)
            token = sums
    block = kernel_call(
        sums_kernel, array(n_member * share, width, BF16), sums, *from_both, name="span_sums", after=(token,)
    )

    early_own, early_sent = over_cores([*parts[:EARLY], block], "early")
    from_mp = swap(early_sent, "mp")
    make_part(EARLY, early_sent)
    own, sent = over_cores(parts[EARLY:], "late")
    *ready, span_grad = kernel_call(
        add_kernel, (array(GROUP, depth, BF16),) * 4, early_own, from_mp, name="early_add", after=(sent,)
    )

    turned = kernel_call(
        turn_kernel, (array(GROUP, depth, BF16),) * n_seq, own, swap(sent, "mp"), *ready, name="turn"
    )
    arrived = [turned[0]]
    for turn in range(1, n_seq):
        pairs = [(i, (i + turn) % n_seq) for i in range(n_seq)]
        arrived.append(lax.ppermute(turned[turn], "seq", pairs))
    main_out = kernel_call(join_kernel, array(share, main_width, BF16), *arrived, name="join")
    return (main_out, span_grad)


def solution(mesh):
    spread = P(("groups", "seq", "mp", "rep"), None)
    weight = P("seq", ("mp", "rep"))
    placed = (spread, spread, P("groups"), P(), P(), P(), P(), P(), weight, weight, weight)
    return jax.shard_map(
        local, mesh=mesh, in_specs=placed, out_specs=(spread, spread), check_vma=False
    )
```

```python
import functools

import jax
import jax.numpy as jnp
from jax import lax
from jax.experimental import pallas as pl
from jax.experimental.pallas import tpu as pltpu
from jax.sharding import PartitionSpec as P

HEAD = 128
WINDOW = 128
CAP = 64
LANE = 24
LANE_ROWS = 32
GROUP = 32
VMEM = pl.BlockSpec(memory_space=pltpu.VMEM)
ANY = pl.BlockSpec(memory_space=pl.ANY)
COST = {
    "plan": 20_000_000_000,
    "tick0": 4_000_000_000,
    "tick1": 2_000_000_000,
    "tick2": 2_000_000_000,
    "tick3": 2_000_000_000,
    "tickz": 2_000_000_000,
    "early_core": 4_000_000_000,
    "encode": 20_000_000_000,
    "hidden0": 2_000_000_000,
}
CHUNKS = ((0, 3), (3, 7), (7, 12), (12, 16))
EARLY = 3
PART = ("seq", "mp", "rep")
MEMBER = ("mp", "rep")
F32 = jnp.float32
BF16 = jnp.bfloat16


def dot(a, b):
    return jnp.dot(a, b, preferred_element_type=F32)


def dot_t(a, b):
    return lax.dot_general(a, b, (((1,), (1,)), ((), ())), preferred_element_type=F32)


def is_direct():
    return lax.axis_size("seq") == 4 and lax.axis_size("mp") == 2 and lax.axis_size("rep") == 2


def swap(value, axis):
    return lax.ppermute(value, axis, [(0, 1), (1, 0)])


def kernel_call(kernel, out_shape, *operands, name, after=()):
    count = len(operands)
    body = lambda *refs: kernel(*refs[:count], *refs[count + len(after) :])
    return pl.pallas_call(
        body,
        out_shape=out_shape,
        in_specs=[VMEM] * count + [ANY] * len(after),
        out_specs=jax.tree.map(lambda _: VMEM, out_shape),
        compiler_params=pltpu.CompilerParams(vmem_limit_bytes=24 << 20),
        cost_estimate=pl.CostEstimate(flops=COST.get(name, 0), bytes_accessed=0, transcendentals=0),
        name=name,
    )(*operands, *after)


def tick(name, *after):
    def kernel(out_ref):
        out_ref[...] = jnp.zeros_like(out_ref)

    return kernel_call(kernel, array(8, 128, F32), name=name, after=after)


def tie(values, token):
    return lax.optimization_barrier((values, token))


def array(rows, columns, dtype):
    return jax.ShapeDtypeStruct((rows, columns), dtype)


def rms_scale(values, gain):
    return values * lax.rsqrt(jnp.mean(values * values, axis=-1, keepdims=True) + 1e-05) * gain


def encode(x, halo, begin, sel, q_at, enc_gain, w_qkv, w_out):
    length, width = x.shape
    heads = width // HEAD
    both = jnp.concatenate([halo, x], axis=0)
    normed = rms_scale(both.astype(F32), enc_gain).astype(BF16)
    picked = dot(sel, normed[length:]).astype(BF16)
    queries = dot(picked, w_qkv[:, :width]).astype(BF16)
    keyval = dot(normed, w_qkv[:, width:]).astype(BF16)
    k_at = jnp.arange(2 * length, dtype=jnp.int32) - length
    allowed = (
        (k_at[None, :] <= q_at[:, None])
        & (k_at[None, :] > q_at[:, None] - WINDOW)
        & (k_at[None, :] + begin >= 0)
    )
    q_heads = queries.reshape(CAP, heads, HEAD)
    k_heads = keyval[:, :width].reshape(2 * length, heads, HEAD)
    v_heads = keyval[:, width:].reshape(2 * length, heads, HEAD)
    scores = jnp.einsum("qhd,khd->hqk", q_heads, k_heads, preferred_element_type=F32)
    scores = jnp.where(allowed[None], scores / jnp.sqrt(F32(HEAD)), F32(-1e30))
    probs = jax.nn.softmax(scores, axis=-1).astype(BF16)
    mixed = jnp.einsum("hqk,khd->qhd", probs, v_heads, preferred_element_type=F32)
    attended = mixed.reshape(CAP, width).astype(BF16)
    return (dot(sel, x) + dot(attended, w_out)).astype(BF16)


def sum_of_spans(cotangent, span_index):
    n_member = lax.axis_size(MEMBER)
    n_seq = lax.axis_size("seq")
    owner = lax.axis_index("seq")
    length, width = cotangent.shape
    span_own = 32 * n_member
    lowest, highest = span_index[0], span_index[length - 1]
    slot_ids = jnp.arange(CAP, dtype=jnp.int32)
    onehot = (span_index[None, :] - lowest == slot_ids[:, None]).astype(BF16)
    pieces = dot(onehot, cotangent).astype(BF16)
    span_ids = lowest + slot_ids
    valid = (span_ids <= highest)[None, :]
    lane_ids = jnp.arange(LANE, dtype=jnp.int32)
    row_ids = jnp.arange(span_own, dtype=jnp.int32)

    def choose(targets):
        return dot(((targets[:, None] == span_ids[None, :]) & valid).astype(BF16), pieces)

    to_before = choose(owner * span_own - LANE + lane_ids).astype(BF16)
    to_after = choose((owner + 1) * span_own + lane_ids).astype(BF16)
    up = [(i, i + 1) for i in range(n_seq - 1)]
    down = [(i + 1, i) for i in range(n_seq - 1)]
    from_before = lax.ppermute(to_after, "seq", up).astype(F32)
    from_after = lax.ppermute(to_before, "seq", down).astype(F32)
    block = choose(owner * span_own + row_ids)
    block = jnp.concatenate(
        [block[:LANE] + from_before, block[LANE:-LANE], block[-LANE:] + from_after], axis=0
    )
    sent = block.astype(BF16).reshape(n_member, span_own // n_member, width)
    got = lax.all_to_all(sent, MEMBER, 0, 0, tiled=True)
    return jnp.sum(got.astype(F32), axis=0).astype(BF16)


def relay(value):
    return lax.ppermute(value, "seq", [(2, 1)]), lax.ppermute(value, "seq", [(2, 3)])


def lanes_kernel(member_ref, cotangent_ref, own_ref, before_ref, after_ref):
    own = own_ref.shape[0]
    sums = dot(member_ref[...], cotangent_ref[...]).astype(BF16)
    own_ref[...] = sums[:own]
    before_ref[...] = sums[own : own + LANE_ROWS]
    after_ref[...] = sums[own + LANE_ROWS :]


def pad_kernel(pad_ref, gain_ref, gate_ref, up_ref, out_ref):
    seq = lax.axis_index("seq")
    depth = gate_ref.shape[0]
    pad = pad_ref[:, pl.ds(pl.multiple_of(jnp.maximum(seq - 1, 0) * depth, depth), depth)]
    gain = gain_ref[:, pl.ds(pl.multiple_of(seq * depth, depth), depth)]
    high, low = split_high_low(jnp.broadcast_to(pad * gain, (8, depth)))
    both = jnp.concatenate([high, low], axis=0)
    for at, weight_ref in enumerate((gate_ref, up_ref)):
        terms = dot(both, weight_ref[...])
        out_ref[at : at + 1] = jnp.where(seq == 0, 0.0, terms[:1] + terms[8:9])


def plan_kernel(starts_ref, sel_ref, bias_ref, place_ref, member_ref):
    owner, core = lax.axis_index("seq"), lax.axis_index("rep")
    here_member = lax.axis_index("mp") * 2 + core
    device = owner * 4 + here_member
    n_span = starts_ref.shape[1]
    length = sel_ref.shape[1]
    begin = device * length
    row = starts_ref[...]
    column = jnp.transpose(jnp.broadcast_to(row, (length, n_span)))
    here = begin + lax.broadcasted_iota(jnp.int32, (n_span, length), 1)
    earlier = jnp.sum(jnp.where(column < here, 1.0, 0.0), axis=0, keepdims=True).astype(jnp.int32)
    start = jnp.sum(jnp.where(column == here, 1.0, 0.0), axis=0, keepdims=True).astype(jnp.int32)
    slot = lax.broadcasted_iota(jnp.int32, (CAP, length), 0)
    picked = (earlier - earlier[:, :1] == slot) & (start > 0)
    picked = jnp.where(picked, 1.0, 0.0)
    sel_ref[...] = picked.astype(BF16)
    place_in = lax.broadcasted_iota(jnp.int32, (CAP, length), 1).astype(F32)
    q_at = jnp.sum(picked * place_in, axis=1, keepdims=True).astype(jnp.int32)
    k_at = lax.broadcasted_iota(jnp.int32, (CAP, 2 * length), 1) - length
    allowed = (k_at <= q_at) & (k_at > q_at - WINDOW) & (k_at + begin >= 0)
    bias_ref[...] = jnp.where(allowed, 0.0, -1e30)

    span_index = earlier + start - 1
    n_row = member_ref.shape[0]
    own = n_row - 2 * LANE_ROWS
    at = lax.broadcasted_iota(jnp.int32, (n_row, length), 0)
    target = jnp.where(
        at < own, owner * own + at, jnp.where(at < own + LANE_ROWS, owner * own - LANE_ROWS - own, owner * own - LANE_ROWS) + at
    )
    member_ref[...] = jnp.where(span_index == target, 1.0, 0.0).astype(BF16)

    block = column[:, :1] // length
    before = jnp.sum(jnp.where(row < block * length, 1.0, 0.0), axis=1, keepdims=True).astype(jnp.int32)
    span = lax.broadcasted_iota(jnp.int32, (n_span, 1), 0)
    near = jnp.minimum((span // 32 + 1) // 4, 3)
    turned = (block % 4) ^ here_member
    turned = (turned % 2) * 2 + turned // 2
    lies = ((block // 4 - near + 1) * 4 + turned) * CAP + span - before
    lanes = lax.broadcasted_iota(jnp.int32, place_ref.shape, 1)
    place_ref[...] = jnp.where(lanes == lies, 1.0, 0.0).astype(BF16)


def plan(boundaries, length, span_own):
    n_span = boundaries.shape[0]
    return kernel_call(
        plan_kernel,
        (
            array(CAP, length, BF16),
            array(CAP, 2 * length, F32),
            array(n_span, 8 * CAP, BF16),
            array(span_own + 2 * LANE_ROWS, length, BF16),
        ),
        boundaries.reshape(1, n_span),
        name="plan",
    )


def project(normed, qkv_ref, at):
    width = normed.shape[1]
    wide = 2 * HEAD
    keys = dot(normed, qkv_ref[:, width + at : width + at + wide]).astype(BF16)
    values = dot(normed, qkv_ref[:, 2 * width + at : 2 * width + at + wide]).astype(BF16)
    return keys, values


def own_kernel(x_ref, sel_ref, gain_ref, qkv_ref, q_ref, kv_ref):
    width = x_ref.shape[1]
    wide = 2 * HEAD
    normed = rms_scale(x_ref[...].astype(F32), gain_ref[...]).astype(BF16)
    picked = dot(sel_ref[...], normed).astype(BF16)
    for at in range(0, width, wide):
        q_ref[:, at : at + wide] = dot(picked, qkv_ref[:, at : at + wide]).astype(BF16)
        keys, values = project(normed, qkv_ref, at)
        kv_ref[:, at : at + wide] = keys
        kv_ref[:, width + at : width + at + wide] = values


def encode_kernel(x_ref, halo_ref, sel_ref, bias_ref, gain_ref, qkv_ref, o_ref, q_ref, kv_ref, out_ref):
    width = x_ref.shape[1]
    wide = 2 * HEAD
    sel = sel_ref[...]
    bias = bias_ref[...]
    normed = rms_scale(halo_ref[...].astype(F32), gain_ref[...]).astype(BF16)
    mixed = []
    for at in range(0, width, wide):
        queries = q_ref[:, at : at + wide]
        keys, values = project(normed, qkv_ref, at)
        keys = jnp.concatenate([keys, kv_ref[:, at : at + wide]], axis=0)
        values = jnp.concatenate([values, kv_ref[:, width + at : width + at + wide]], axis=0)
        for head in range(0, wide, HEAD):
            part = slice(head, head + HEAD)
            scores = dot_t(queries[:, part], keys[:, part]) * (HEAD**-0.5) + bias
            probs = jnp.exp(scores - jnp.max(scores, axis=1, keepdims=True))
            probs = (probs / jnp.sum(probs, axis=1, keepdims=True)).astype(BF16)
            mixed.append(dot(probs, values[:, part]).astype(BF16))
    total = dot(sel, x_ref[...]) + dot(jnp.concatenate(mixed, axis=1), o_ref[...])
    out_ref[...] = total.astype(BF16)


def terms_kernel(*refs):
    *in_refs, out_ref = refs
    out_ref[...] = sum(ref[...] for ref in in_refs)


def near_of(group):
    return min((group + 1) // 4, 3)


def hidden_kernel(low, high, place_ref, *refs):
    base = max(near_of(low) - 1, 0)
    count = 4 * (near_of(high - 1) - base + 1)
    block_refs, refs = refs[:count], refs[count:]
    pad_ref, gain_ref, gate_ref, up_ref, term_ref, hidden_ref, row_ref = refs
    width = row_ref.shape[1]
    row = []
    while low < high:
        near = near_of(low)
        end = min(high, 4 * near + 3) if near < 3 else high
        total = 0.0
        for seq in range(max(near - 1, 0), near + 1):
            blocks = jnp.concatenate([ref[...] for ref in block_refs[(seq - base) * 4 : (seq - base) * 4 + 4]], axis=0)
            lanes = (seq - near + 1) * 4 * CAP
            total += dot(place_ref[low * GROUP : end * GROUP, lanes : lanes + 4 * CAP], blocks)
        row.append(total)
        low = end
    row = jnp.concatenate(row, axis=0)
    pad = pad_ref[...]
    total = jnp.sum(row * row, axis=1, keepdims=True) + jnp.sum(pad * pad)
    scale = lax.rsqrt(total / (width + pad.shape[1]) + 1e-05)
    main_in = (row * scale * gain_ref[:, :width]).astype(BF16)
    terms = term_ref[...]
    gate = dot(main_in, gate_ref[...]) + scale * terms[:1]
    upward = dot(main_in, up_ref[...]) + scale * terms[1:2]
    hidden_ref[...] = (gate / (1.0 + jnp.exp(-gate)) * upward).astype(BF16)
    row_ref[...] = row.astype(BF16)


def hidden_at_zero(*args):
    pl.when(lax.axis_index("seq") == 0)(lambda: hidden_kernel(*args))


def down_kernel(zero_ref, one_ref, two_ref, three_ref, down_ref, row_ref, pad_ref, out_ref):
    seq = lax.axis_index("seq")
    depth = down_ref.shape[0]
    low = jnp.where(seq == 0, zero_ref[...], one_ref[...])
    high = jnp.where(seq == 2, two_ref[...], three_ref[...])
    partial = dot_t(jnp.where(seq < 2, low, high), down_ref[...])
    pad = pad_ref[:, pl.ds(pl.multiple_of(jnp.maximum(seq - 1, 0) * depth, depth), depth)]
    wide = jnp.where(seq == 0, row_ref[...].astype(F32), pad)
    first = (lax.axis_index("mp") == 0) & (lax.axis_index("rep") == 0)
    out_ref[...] = partial + jnp.where(first, wide, 0.0)


def groups_of(refs):
    return [ref.at[at : at + GROUP] for ref in refs for at in range(0, ref.shape[0], GROUP)]


def core_step_kernel(count, *refs):
    core = lax.axis_index("rep")
    groups = groups_of(refs[:count])
    outs = groups_of(refs[count:])
    for at, out in enumerate(outs):
        out[...] = jnp.where(core == 0, groups[2 * at + 1][...], groups[2 * at][...]).astype(BF16)


def chip_step_kernel(count, *refs):
    *came_refs, own_ref, other_ref = refs[count:]
    core, chip = lax.axis_index("rep"), lax.axis_index("mp")
    groups = groups_of(refs[:count])
    came = groups_of(came_refs)
    for at in range(len(groups) // 4):
        first, second = (
            jnp.where(core == 0, groups[4 * at + 2 * i][...], groups[4 * at + 2 * i + 1][...]).astype(F32)
            + came[2 * at + i][...].astype(F32)
            for i in range(2)
        )
        rows = slice(at * GROUP, (at + 1) * GROUP)
        own_ref[rows] = jnp.where(chip == 0, first, second)
        other_ref[rows] = jnp.where(chip == 0, second, first).astype(BF16)


def add_kernel(own_ref, came_ref, *out_refs):
    for at, out_ref in enumerate(out_refs):
        rows = slice(at * GROUP, (at + 1) * GROUP)
        out_ref[...] = (own_ref[rows] + came_ref[rows].astype(F32)).astype(BF16)


def sums_kernel(sums_ref, before_ref, after_ref, out_ref):
    own = out_ref.shape[0]
    out_ref[...] = sums_ref[:own]
    out_ref[:LANE_ROWS] = (sums_ref[:LANE_ROWS].astype(F32) + before_ref[...].astype(F32)).astype(BF16)
    last = slice(own - LANE_ROWS, own)
    out_ref[last] = (sums_ref[last].astype(F32) + after_ref[...].astype(F32)).astype(BF16)


def turn_kernel(own_ref, came_ref, *refs):
    early_refs, out_refs = refs[:3], refs[3:]
    seq = lax.axis_index("seq")
    late = (own_ref[...] + came_ref[...].astype(F32)).astype(BF16)
    groups = [ref[...] for ref in early_refs] + [late]
    for turn, out_ref in enumerate(out_refs):
        owner = (seq + turn) % 4
        value = groups[3]
        for at in range(3):
            value = jnp.where(owner == at, groups[at], value)
        out_ref[...] = value


def join_kernel(*refs):
    *in_refs, out_ref = refs
    seq = lax.axis_index("seq")
    depth = in_refs[0].shape[1]
    for maker in range(4):
        turn = (seq - maker + 4) % 4
        value = in_refs[3][...]
        for at in range(3):
            value = jnp.where(turn == at, in_refs[at][...], value)
        out_ref[:, maker * depth : (maker + 1) * depth] = value


def split_high_low(values):
    high = values.astype(BF16)
    return high, (values - high.astype(F32)).astype(BF16)


def block_first(boundaries, blocks, length):
    edges = jnp.stack([blocks, blocks + 1]) * length
    return jnp.sum((boundaries[:, None, None] < edges[None]).astype(jnp.int32), axis=0)


def place(first, span_ids):
    slots = jnp.arange(CAP, dtype=jnp.int32)
    held = first[0][:, None] + slots[None, :]
    held = jnp.where(held < first[1][:, None], held, -1).reshape(-1)
    return (span_ids[:, None] == held[None, :]).astype(BF16)


def local(
    byte_states,
    cotangent,
    boundaries,
    enc_gain,
    w_qkv,
    w_out,
    pad_vector,
    main_gain,
    gate_w,
    up_w,
    down_t,
):
    n_member = lax.axis_size(MEMBER)
    n_seq = lax.axis_size("seq")
    n_dev = n_seq * n_member
    seq = lax.axis_index("seq")
    device = lax.axis_index(PART)
    length, width = byte_states.shape
    depth, columns = gate_w.shape
    main_width = depth * n_seq
    n_span = boundaries.shape[0]
    share = n_span // n_dev
    begin = device * length

    shift = [(i, i + 1) for i in range(n_dev - 1)]
    halo = lax.ppermute(byte_states, PART, shift)

    direct = is_direct() and depth == width
    if direct:
        pad_row, gain_row = pad_vector.reshape(1, -1), main_gain.reshape(1, -1)
        sel, bias, where, member_of = plan(boundaries, length, n_member * share)
        pad_terms = kernel_call(
            pad_kernel, array(2, columns, F32), pad_row, gain_row, gate_w, up_w, name="pad_terms", after=(sel,)
        )
        own = kernel_call(
            own_kernel,
            (array(CAP, width, BF16), array(length, 2 * width, BF16)),
            byte_states,
            sel,
            enc_gain.reshape(1, width),
            w_qkv,
            name="own",
            after=(pad_terms,),
        )
        rows = kernel_call(
            encode_kernel,
            array(CAP, width, BF16),
            byte_states,
            halo,
            sel,
            bias,
            enc_gain.reshape(1, width),
            w_qkv,
            w_out,
            *own,
            name="encode",
            after=(pad_terms,),
        )
    else:
        wide_gain = main_gain[width:]
        pad_in = jnp.concatenate([jnp.zeros((width,), F32), pad_vector * wide_gain])
        pad_here = lax.dynamic_slice_in_dim(pad_in, seq * depth, depth, 0)
        pad_rows = jnp.stack(split_high_low(pad_here) * 4)
        pad_terms = jnp.concatenate([dot(pad_rows, gate_w), dot(pad_rows, up_w)], axis=1)
        pad_terms = pad_terms[:1] + pad_terms[1:2]

        places = jnp.arange(length, dtype=jnp.int32)
        earlier = jnp.sum((boundaries[:, None] < begin + places[None, :]).astype(jnp.int32), axis=0)
        starts = jnp.sum((boundaries[:, None] == begin + places[None, :]).astype(jnp.int32), axis=0)
        slot_ids = jnp.arange(CAP, dtype=jnp.int32)
        picks = (earlier - earlier[0] == slot_ids[:, None]) & (starts > 0)
        q_at = jnp.sum(jnp.where(picks, places[None, :], 0), axis=1)
        sel = picks.astype(BF16)
        span_grad = sum_of_spans(cotangent, earlier + starts - 1)
        rows = encode(byte_states, halo, begin, sel, q_at, enc_gain, w_qkv, w_out)

    gain_rows = main_gain[:width]
    pad_square = jnp.sum(pad_vector * pad_vector)

    def scaled(compact):
        squares = jnp.sum(compact * compact, axis=1, keepdims=True) + pad_square
        scale = lax.rsqrt(squares / main_width + 1e-05)
        return scale, (compact * scale * gain_rows).astype(BF16)

    if not direct:
        gathered = lax.all_gather(rows, PART, axis=0, tiled=True)
        order = jnp.arange(n_span, dtype=jnp.int32).reshape(n_seq, n_member, share)
        order = order.transpose(1, 0, 2).reshape(-1)
        first = block_first(boundaries, jnp.arange(n_dev, dtype=jnp.int32), length)
        compact = dot(place(first, order), gathered)
        scale, main_in = scaled(compact)
        padded = jnp.pad(main_in, ((0, 0), (0, main_width - width)))
        here = lax.dynamic_slice_in_dim(padded, seq * depth, depth, 1)
        gate = dot(here, gate_w) + scale * pad_terms[:, :columns]
        upward = dot(here, up_w) + scale * pad_terms[:, columns:]
        gate, upward = lax.psum((gate, upward), "seq")
        hidden = (jax.nn.silu(gate) * upward).astype(BF16)
        partial = dot_t(hidden, down_t).astype(BF16).reshape(n_member, n_seq * share, depth)
        got = lax.all_to_all(partial, MEMBER, 0, 0, tiled=True)
        summed = jnp.sum(got.astype(F32), axis=0)
        member = lax.axis_index(MEMBER)
        mine = lax.dynamic_slice_in_dim(compact, member * n_seq * share, n_seq * share, 0)
        wide = jnp.concatenate(
            [mine, jnp.broadcast_to(pad_vector, (n_seq * share, main_width - width))], axis=1
        )
        residual = lax.dynamic_slice_in_dim(wide, seq * depth, depth, 1)
        done = (summed + residual).astype(BF16).reshape(n_seq, share, depth)
        spread = lax.all_to_all(done, "seq", 0, 0, tiled=True)
        main_out = spread.transpose(1, 0, 2).reshape(share, main_width)
        return (main_out, span_grad)

    terms = [lax.ppermute(pad_terms, "seq", [(j, 0)]) for j in range(n_seq - 1, 0, -1)]
    terms = kernel_call(terms_kernel, array(2, columns, F32), *terms, name="terms", after=(rows,))
    rows, terms = tie(rows, terms)
    def to_members(value):
        from_chip = swap(value, "mp")
        return value, from_chip, swap(value, "rep"), swap(from_chip, "rep")

    came = [lax.ppermute(rows, "seq", [(j, 0)]) for j in range(1, n_seq)]
    across = lax.ppermute(rows, MEMBER, [(j, 3 - j) for j in range(4)])
    planes = [(rows, swap(rows, "mp"), swap(rows, "rep"), across)]

    def over_cores(values, name):
        quarters = sum(value.shape[0] for value in values) // GROUP // 4
        sent = kernel_call(
            functools.partial(core_step_kernel, len(values)),
            (array(2 * GROUP, depth, BF16),) * quarters,
            *values,
            name=name + "_core",
        )
        return kernel_call(
            functools.partial(chip_step_kernel, len(values)),
            (array(quarters * GROUP, depth, F32), array(quarters * GROUP, depth, BF16)),
            *values,
            *(swap(value, "rep") for value in sent),
            name=name + "_chip",
        )

    hiddens, row_parts, relayed, spread, parts = [], [], [], [], []

    def make_hidden(index, *after):
        low, high = CHUNKS[index]
        halves = [block for plane in planes[max(near_of(low) - 1, 0) : near_of(high - 1) + 1] for block in plane]
        count = (high - low) * share
        hidden, row = kernel_call(
            functools.partial(hidden_at_zero, low, high),
            (array(count, columns, BF16), array(count, width, BF16)),
            where,
            *halves,
            pad_row,
            gain_row,
            gate_w,
            up_w,
            terms,
            name=f"hidden{index}",
            after=after,
        )
        hiddens.append(hidden)
        row_parts.append(row)
        relayed.append(lax.ppermute(hidden, "seq", [(0, 2)]))

    def make_part(index, *after):
        at_one, at_three = spread[index]
        count = row_parts[index].shape[0]
        parts.append(
            kernel_call(
                down_kernel,
                array(count, depth, F32),
                hiddens[index],
                at_one,
                relayed[index],
                at_three,
                down_t,
                row_parts[index],
                pad_row,
                name=f"down{index}",
                after=after,
            )
        )

    def pass_on(index, token):
        relayed[index], token = tie(relayed[index], token)
        spread.append(relay(relayed[index]))
        return relayed[index], token

    value, token = tie(came[0], rows)
    planes.append(to_members(value))
    make_hidden(0, token)
    token = tick("tickz", hiddens[0])
    later = []
    for value in came[1:]:
        value, token = tie(value, token)
        later.append((value, swap(value, "mp"), swap(value, "rep")))
    make_hidden(1, token)
    token = hiddens[1]
    for value, from_chip, from_core in later:
        from_chip, token = tie(from_chip, token)
        planes.append((value, from_chip, from_core, swap(from_chip, "rep")))
    make_hidden(2, token)
    make_hidden(3, hiddens[2])
    token = hiddens[3]
    for index in range(len(CHUNKS)):
        arrived, token = pass_on(index, token)
        token = tick(f"tick{index}", token)
        if index:
            make_part(index - 1, token, arrived)
            token = parts[-1]
        if index == 1:
            sums, to_before, to_after = kernel_call(
                lanes_kernel,
                (array(n_member * share, width, BF16),) + (array(LANE_ROWS, width, BF16),) * 2,
                member_of,
                cotangent,
                name="lanes",
                after=(token,),
            )
            up = [(i, i + 1) for i in range(n_seq - 1)]
            down = [(i + 1, i) for i in range(n_seq - 1)]
            from_both = lax.ppermute(to_after, "seq", up), lax.ppermute(to_before, "seq", down)
            token = sums
    block = kernel_call(
        sums_kernel, array(n_member * share, width, BF16), sums, *from_both, name="span_sums", after=(token,)
    )

    early_own, early_sent = over_cores([*parts[:EARLY], block], "early")
    from_mp = swap(early_sent, "mp")
    make_part(EARLY, early_sent)
    own, sent = over_cores(parts[EARLY:], "late")
    *ready, span_grad = kernel_call(
        add_kernel, (array(GROUP, depth, BF16),) * 4, early_own, from_mp, name="early_add", after=(sent,)
    )

    turned = kernel_call(
        turn_kernel, (array(GROUP, depth, BF16),) * n_seq, own, swap(sent, "mp"), *ready, name="turn"
    )
    arrived = [turned[0]]
    for turn in range(1, n_seq):
        pairs = [(i, (i + turn) % n_seq) for i in range(n_seq)]
        arrived.append(lax.ppermute(turned[turn], "seq", pairs))
    main_out = kernel_call(join_kernel, array(share, main_width, BF16), *arrived, name="join")
    return (main_out, span_grad)


def solution(mesh):
    spread = P(("groups", "seq", "mp", "rep"), None)
    weight = P("seq", ("mp", "rep"))
    placed = (spread, spread, P("groups"), P(), P(), P(), P(), P(), weight, weight, weight)
    return jax.shard_map(
        local, mesh=mesh, in_specs=placed, out_specs=(spread, spread), check_vma=False
    )
```

```python
import functools

import jax
import jax.numpy as jnp
from jax import lax
from jax.experimental import pallas as pl
from jax.experimental.pallas import tpu as pltpu
from jax.sharding import PartitionSpec as P

HEAD = 128
WINDOW = 128
CAP = 64
LANE = 24
LANE_ROWS = 32
GROUP = 32
VMEM = pl.BlockSpec(memory_space=pltpu.VMEM)
ANY = pl.BlockSpec(memory_space=pl.ANY)
COST = {
    "plan": 20_000_000_000,
    "tick0": 4_000_000_000,
    "tick1": 2_000_000_000,
    "tick2": 2_000_000_000,
    "tick3": 2_000_000_000,
    "tickz": 2_000_000_000,
    "early_core": 4_000_000_000,
    "encode": 20_000_000_000,
    "hidden0": 2_000_000_000,
}
CHUNKS = ((0, 3), (3, 7), (7, 12), (12, 16))
EARLY = 3
PART = ("seq", "mp", "rep")
MEMBER = ("mp", "rep")
F32 = jnp.float32
BF16 = jnp.bfloat16


def dot(a, b):
    return jnp.dot(a, b, preferred_element_type=F32)


def dot_t(a, b):
    return lax.dot_general(a, b, (((1,), (1,)), ((), ())), preferred_element_type=F32)


def is_direct():
    return lax.axis_size("seq") == 4 and lax.axis_size("mp") == 2 and lax.axis_size("rep") == 2


def swap(value, axis):
    return lax.ppermute(value, axis, [(0, 1), (1, 0)])


def kernel_call(kernel, out_shape, *operands, name, after=()):
    count = len(operands)
    body = lambda *refs: kernel(*refs[:count], *refs[count + len(after) :])
    return pl.pallas_call(
        body,
        out_shape=out_shape,
        in_specs=[VMEM] * count + [ANY] * len(after),
        out_specs=jax.tree.map(lambda _: VMEM, out_shape),
        compiler_params=pltpu.CompilerParams(vmem_limit_bytes=24 << 20),
        cost_estimate=pl.CostEstimate(flops=COST.get(name, 0), bytes_accessed=0, transcendentals=0),
        name=name,
    )(*operands, *after)


def tick(name, *after):
    def kernel(out_ref):
        out_ref[...] = jnp.zeros_like(out_ref)

    return kernel_call(kernel, array(8, 128, F32), name=name, after=after)


def tie(values, token):
    return lax.optimization_barrier((values, token))


def array(rows, columns, dtype):
    return jax.ShapeDtypeStruct((rows, columns), dtype)


def rms_scale(values, gain):
    return values * lax.rsqrt(jnp.mean(values * values, axis=-1, keepdims=True) + 1e-05) * gain


def encode(x, halo, begin, sel, q_at, enc_gain, w_qkv, w_out):
    length, width = x.shape
    heads = width // HEAD
    both = jnp.concatenate([halo, x], axis=0)
    normed = rms_scale(both.astype(F32), enc_gain).astype(BF16)
    picked = dot(sel, normed[length:]).astype(BF16)
    queries = dot(picked, w_qkv[:, :width]).astype(BF16)
    keyval = dot(normed, w_qkv[:, width:]).astype(BF16)
    k_at = jnp.arange(2 * length, dtype=jnp.int32) - length
    allowed = (
        (k_at[None, :] <= q_at[:, None])
        & (k_at[None, :] > q_at[:, None] - WINDOW)
        & (k_at[None, :] + begin >= 0)
    )
    q_heads = queries.reshape(CAP, heads, HEAD)
    k_heads = keyval[:, :width].reshape(2 * length, heads, HEAD)
    v_heads = keyval[:, width:].reshape(2 * length, heads, HEAD)
    scores = jnp.einsum("qhd,khd->hqk", q_heads, k_heads, preferred_element_type=F32)
    scores = jnp.where(allowed[None], scores / jnp.sqrt(F32(HEAD)), F32(-1e30))
    probs = jax.nn.softmax(scores, axis=-1).astype(BF16)
    mixed = jnp.einsum("hqk,khd->qhd", probs, v_heads, preferred_element_type=F32)
    attended = mixed.reshape(CAP, width).astype(BF16)
    return (dot(sel, x) + dot(attended, w_out)).astype(BF16)


def sum_of_spans(cotangent, span_index):
    n_member = lax.axis_size(MEMBER)
    n_seq = lax.axis_size("seq")
    owner = lax.axis_index("seq")
    length, width = cotangent.shape
    span_own = 32 * n_member
    lowest, highest = span_index[0], span_index[length - 1]
    slot_ids = jnp.arange(CAP, dtype=jnp.int32)
    onehot = (span_index[None, :] - lowest == slot_ids[:, None]).astype(BF16)
    pieces = dot(onehot, cotangent).astype(BF16)
    span_ids = lowest + slot_ids
    valid = (span_ids <= highest)[None, :]
    lane_ids = jnp.arange(LANE, dtype=jnp.int32)
    row_ids = jnp.arange(span_own, dtype=jnp.int32)

    def choose(targets):
        return dot(((targets[:, None] == span_ids[None, :]) & valid).astype(BF16), pieces)

    to_before = choose(owner * span_own - LANE + lane_ids).astype(BF16)
    to_after = choose((owner + 1) * span_own + lane_ids).astype(BF16)
    up = [(i, i + 1) for i in range(n_seq - 1)]
    down = [(i + 1, i) for i in range(n_seq - 1)]
    from_before = lax.ppermute(to_after, "seq", up).astype(F32)
    from_after = lax.ppermute(to_before, "seq", down).astype(F32)
    block = choose(owner * span_own + row_ids)
    block = jnp.concatenate(
        [block[:LANE] + from_before, block[LANE:-LANE], block[-LANE:] + from_after], axis=0
    )
    sent = block.astype(BF16).reshape(n_member, span_own // n_member, width)
    got = lax.all_to_all(sent, MEMBER, 0, 0, tiled=True)
    return jnp.sum(got.astype(F32), axis=0).astype(BF16)


def relay(value):
    return lax.ppermute(value, "seq", [(2, 1)]), lax.ppermute(value, "seq", [(2, 3)])


def lanes_kernel(member_ref, cotangent_ref, own_ref, before_ref, after_ref):
    own = own_ref.shape[0]
    sums = dot(member_ref[...], cotangent_ref[...]).astype(BF16)
    own_ref[...] = sums[:own]
    before_ref[...] = sums[own : own + LANE_ROWS]
    after_ref[...] = sums[own + LANE_ROWS :]


def pad_kernel(pad_ref, gain_ref, gate_ref, up_ref, out_ref):
    seq = lax.axis_index("seq")
    depth = gate_ref.shape[0]
    pad = pad_ref[:, pl.ds(pl.multiple_of(jnp.maximum(seq - 1, 0) * depth, depth), depth)]
    gain = gain_ref[:, pl.ds(pl.multiple_of(seq * depth, depth), depth)]
    high, low = split_high_low(jnp.broadcast_to(pad * gain, (8, depth)))
    both = jnp.concatenate([high, low], axis=0)
    for at, weight_ref in enumerate((gate_ref, up_ref)):
        terms = dot(both, weight_ref[...])
        out_ref[at : at + 1] = jnp.where(seq == 0, 0.0, terms[:1] + terms[8:9])


def plan_kernel(starts_ref, sel_ref, bias_ref, place_ref, member_ref):
    owner, core = lax.axis_index("seq"), lax.axis_index("rep")
    here_member = lax.axis_index("mp") * 2 + core
    device = owner * 4 + here_member
    n_span = starts_ref.shape[1]
    length = sel_ref.shape[1]
    begin = device * length
    row = starts_ref[...]
    column = jnp.transpose(jnp.broadcast_to(row, (length, n_span)))
    here = begin + lax.broadcasted_iota(jnp.int32, (n_span, length), 1)
    earlier = jnp.sum(jnp.where(column < here, 1.0, 0.0), axis=0, keepdims=True).astype(jnp.int32)
    start = jnp.sum(jnp.where(column == here, 1.0, 0.0), axis=0, keepdims=True).astype(jnp.int32)
    slot = lax.broadcasted_iota(jnp.int32, (CAP, length), 0)
    picked = (earlier - earlier[:, :1] == slot) & (start > 0)
    picked = jnp.where(picked, 1.0, 0.0)
    sel_ref[...] = picked.astype(BF16)
    place_in = lax.broadcasted_iota(jnp.int32, (CAP, length), 1).astype(F32)
    q_at = jnp.sum(picked * place_in, axis=1, keepdims=True).astype(jnp.int32)
    k_at = lax.broadcasted_iota(jnp.int32, (CAP, 2 * length), 1) - length
    allowed = (k_at <= q_at) & (k_at > q_at - WINDOW) & (k_at + begin >= 0)
    bias_ref[...] = jnp.where(allowed, 0.0, -1e30)

    span_index = earlier + start - 1
    n_row = member_ref.shape[0]
    own = n_row - 2 * LANE_ROWS
    at = lax.broadcasted_iota(jnp.int32, (n_row, length), 0)
    target = jnp.where(
        at < own, owner * own + at, jnp.where(at < own + LANE_ROWS, owner * own - LANE_ROWS - own, owner * own - LANE_ROWS) + at
    )
    member_ref[...] = jnp.where(span_index == target, 1.0, 0.0).astype(BF16)

    block = column[:, :1] // length
    before = jnp.sum(jnp.where(row < block * length, 1.0, 0.0), axis=1, keepdims=True).astype(jnp.int32)
    span = lax.broadcasted_iota(jnp.int32, (n_span, 1), 0)
    near = jnp.minimum((span // 32 + 1) // 4, 3)
    turned = (block % 4) ^ here_member
    turned = (turned % 2) * 2 + turned // 2
    lies = ((block // 4 - near + 1) * 4 + turned) * CAP + span - before
    lanes = lax.broadcasted_iota(jnp.int32, place_ref.shape, 1)
    place_ref[...] = jnp.where(lanes == lies, 1.0, 0.0).astype(BF16)


def plan(boundaries, length, span_own):
    n_span = boundaries.shape[0]
    return kernel_call(
        plan_kernel,
        (
            array(CAP, length, BF16),
            array(CAP, 2 * length, F32),
            array(n_span, 8 * CAP, BF16),
            array(span_own + 2 * LANE_ROWS, length, BF16),
        ),
        boundaries.reshape(1, n_span),
        name="plan",
    )


def project(normed, qkv_ref, at):
    width = normed.shape[1]
    wide = 2 * HEAD
    keys = dot(normed, qkv_ref[:, width + at : width + at + wide]).astype(BF16)
    values = dot(normed, qkv_ref[:, 2 * width + at : 2 * width + at + wide]).astype(BF16)
    return keys, values


def own_kernel(x_ref, sel_ref, gain_ref, qkv_ref, q_ref, kv_ref):
    width = x_ref.shape[1]
    wide = 2 * HEAD
    normed = rms_scale(x_ref[...].astype(F32), gain_ref[...]).astype(BF16)
    picked = dot(sel_ref[...], normed).astype(BF16)
    for at in range(0, width, wide):
        q_ref[:, at : at + wide] = dot(picked, qkv_ref[:, at : at + wide]).astype(BF16)
        keys, values = project(normed, qkv_ref, at)
        kv_ref[:, at : at + wide] = keys
        kv_ref[:, width + at : width + at + wide] = values


def encode_kernel(x_ref, halo_ref, sel_ref, bias_ref, gain_ref, qkv_ref, o_ref, q_ref, kv_ref, out_ref):
    width = x_ref.shape[1]
    wide = 2 * HEAD
    sel = sel_ref[...]
    bias = bias_ref[...]
    normed = rms_scale(halo_ref[...].astype(F32), gain_ref[...]).astype(BF16)
    mixed = []
    for at in range(0, width, wide):
        queries = q_ref[:, at : at + wide]
        keys, values = project(normed, qkv_ref, at)
        keys = jnp.concatenate([keys, kv_ref[:, at : at + wide]], axis=0)
        values = jnp.concatenate([values, kv_ref[:, width + at : width + at + wide]], axis=0)
        for head in range(0, wide, HEAD):
            part = slice(head, head + HEAD)
            scores = dot_t(queries[:, part], keys[:, part]) * (HEAD**-0.5) + bias
            probs = jnp.exp(scores - jnp.max(scores, axis=1, keepdims=True))
            probs = (probs / jnp.sum(probs, axis=1, keepdims=True)).astype(BF16)
            mixed.append(dot(probs, values[:, part]).astype(BF16))
    total = dot(sel, x_ref[...]) + dot(jnp.concatenate(mixed, axis=1), o_ref[...])
    out_ref[...] = total.astype(BF16)


def terms_kernel(*refs):
    *in_refs, out_ref = refs
    out_ref[...] = sum(ref[...] for ref in in_refs)


def near_of(group):
    return min((group + 1) // 4, 3)


def hidden_kernel(low, high, place_ref, *refs):
    base = max(near_of(low) - 1, 0)
    count = 4 * (near_of(high - 1) - base + 1)
    block_refs, refs = refs[:count], refs[count:]
    pad_ref, gain_ref, gate_ref, up_ref, term_ref, hidden_ref, row_ref = refs
    width = row_ref.shape[1]
    row = []
    while low < high:
        near = near_of(low)
        end = min(high, 4 * near + 3) if near < 3 else high
        total = 0.0
        for seq in range(max(near - 1, 0), near + 1):
            blocks = jnp.concatenate([ref[...] for ref in block_refs[(seq - base) * 4 : (seq - base) * 4 + 4]], axis=0)
            lanes = (seq - near + 1) * 4 * CAP
            total += dot(place_ref[low * GROUP : end * GROUP, lanes : lanes + 4 * CAP], blocks)
        row.append(total)
        low = end
    row = jnp.concatenate(row, axis=0)
    pad = pad_ref[...]
    total = jnp.sum(row * row, axis=1, keepdims=True) + jnp.sum(pad * pad)
    scale = lax.rsqrt(total / (width + pad.shape[1]) + 1e-05)
    main_in = (row * scale * gain_ref[:, :width]).astype(BF16)
    terms = term_ref[...]
    gate = dot(main_in, gate_ref[...]) + scale * terms[:1]
    upward = dot(main_in, up_ref[...]) + scale * terms[1:2]
    hidden_ref[...] = (gate / (1.0 + jnp.exp(-gate)) * upward).astype(BF16)
    row_ref[...] = row.astype(BF16)


def hidden_at_zero(*args):
    pl.when(lax.axis_index("seq") == 0)(lambda: hidden_kernel(*args))


def down_kernel(zero_ref, one_ref, two_ref, three_ref, down_ref, row_ref, pad_ref, out_ref):
    seq = lax.axis_index("seq")
    depth = down_ref.shape[0]
    low = jnp.where(seq == 0, zero_ref[...], one_ref[...])
    high = jnp.where(seq == 2, two_ref[...], three_ref[...])
    partial = dot_t(jnp.where(seq < 2, low, high), down_ref[...])
    pad = pad_ref[:, pl.ds(pl.multiple_of(jnp.maximum(seq - 1, 0) * depth, depth), depth)]
    wide = jnp.where(seq == 0, row_ref[...].astype(F32), pad)
    first = (lax.axis_index("mp") == 0) & (lax.axis_index("rep") == 0)
    out_ref[...] = partial + jnp.where(first, wide, 0.0)


def groups_of(refs):
    return [ref.at[at : at + GROUP] for ref in refs for at in range(0, ref.shape[0], GROUP)]


def core_step_kernel(count, *refs):
    core = lax.axis_index("rep")
    groups = groups_of(refs[:count])
    outs = groups_of(refs[count:])
    for at, out in enumerate(outs):
        out[...] = jnp.where(core == 0, groups[2 * at + 1][...], groups[2 * at][...]).astype(BF16)


def chip_step_kernel(count, *refs):
    *came_refs, own_ref, other_ref = refs[count:]
    core, chip = lax.axis_index("rep"), lax.axis_index("mp")
    groups = groups_of(refs[:count])
    came = groups_of(came_refs)
    for at in range(len(groups) // 4):
        first, second = (
            jnp.where(core == 0, groups[4 * at + 2 * i][...], groups[4 * at + 2 * i + 1][...]).astype(F32)
            + came[2 * at + i][...].astype(F32)
            for i in range(2)
        )
        rows = slice(at * GROUP, (at + 1) * GROUP)
        own_ref[rows] = jnp.where(chip == 0, first, second)
        other_ref[rows] = jnp.where(chip == 0, second, first).astype(BF16)


def add_kernel(own_ref, came_ref, *out_refs):
    for at, out_ref in enumerate(out_refs):
        rows = slice(at * GROUP, (at + 1) * GROUP)
        out_ref[...] = (own_ref[rows] + came_ref[rows].astype(F32)).astype(BF16)


def sums_kernel(sums_ref, before_ref, after_ref, out_ref):
    own = out_ref.shape[0]
    out_ref[...] = sums_ref[:own]
    out_ref[:LANE_ROWS] = (sums_ref[:LANE_ROWS].astype(F32) + before_ref[...].astype(F32)).astype(BF16)
    last = slice(own - LANE_ROWS, own)
    out_ref[last] = (sums_ref[last].astype(F32) + after_ref[...].astype(F32)).astype(BF16)


def turn_kernel(own_ref, came_ref, *refs):
    early_refs, out_refs = refs[:3], refs[3:]
    seq = lax.axis_index("seq")
    late = (own_ref[...] + came_ref[...].astype(F32)).astype(BF16)
    groups = [ref[...] for ref in early_refs] + [late]
    for turn, out_ref in enumerate(out_refs):
        owner = (seq + turn) % 4
        value = groups[3]
        for at in range(3):
            value = jnp.where(owner == at, groups[at], value)
        out_ref[...] = value


def join_kernel(*refs):
    *in_refs, out_ref = refs
    seq = lax.axis_index("seq")
    depth = in_refs[0].shape[1]
    for maker in range(4):
        turn = (seq - maker + 4) % 4
        value = in_refs[3][...]
        for at in range(3):
            value = jnp.where(turn == at, in_refs[at][...], value)
        out_ref[:, maker * depth : (maker + 1) * depth] = value


def split_high_low(values):
    high = values.astype(BF16)
    return high, (values - high.astype(F32)).astype(BF16)


def block_first(boundaries, blocks, length):
    edges = jnp.stack([blocks, blocks + 1]) * length
    return jnp.sum((boundaries[:, None, None] < edges[None]).astype(jnp.int32), axis=0)


def place(first, span_ids):
    slots = jnp.arange(CAP, dtype=jnp.int32)
    held = first[0][:, None] + slots[None, :]
    held = jnp.where(held < first[1][:, None], held, -1).reshape(-1)
    return (span_ids[:, None] == held[None, :]).astype(BF16)


def local(
    byte_states,
    cotangent,
    boundaries,
    enc_gain,
    w_qkv,
    w_out,
    pad_vector,
    main_gain,
    gate_w,
    up_w,
    down_t,
):
    n_member = lax.axis_size(MEMBER)
    n_seq = lax.axis_size("seq")
    n_dev = n_seq * n_member
    seq = lax.axis_index("seq")
    device = lax.axis_index(PART)
    length, width = byte_states.shape
    depth, columns = gate_w.shape
    main_width = depth * n_seq
    n_span = boundaries.shape[0]
    share = n_span // n_dev
    begin = device * length

    shift = [(i, i + 1) for i in range(n_dev - 1)]
    halo = lax.ppermute(byte_states, PART, shift)

    direct = is_direct() and depth == width
    if direct:
        pad_row, gain_row = pad_vector.reshape(1, -1), main_gain.reshape(1, -1)
        sel, bias, where, member_of = plan(boundaries, length, n_member * share)
        pad_terms = kernel_call(
            pad_kernel, array(2, columns, F32), pad_row, gain_row, gate_w, up_w, name="pad_terms", after=(sel,)
        )
        own = kernel_call(
            own_kernel,
            (array(CAP, width, BF16), array(length, 2 * width, BF16)),
            byte_states,
            sel,
            enc_gain.reshape(1, width),
            w_qkv,
            name="own",
            after=(pad_terms,),
        )
        rows = kernel_call(
            encode_kernel,
            array(CAP, width, BF16),
            byte_states,
            halo,
            sel,
            bias,
            enc_gain.reshape(1, width),
            w_qkv,
            w_out,
            *own,
            name="encode",
            after=(pad_terms,),
        )
    else:
        wide_gain = main_gain[width:]
        pad_in = jnp.concatenate([jnp.zeros((width,), F32), pad_vector * wide_gain])
        pad_here = lax.dynamic_slice_in_dim(pad_in, seq * depth, depth, 0)
        pad_rows = jnp.stack(split_high_low(pad_here) * 4)
        pad_terms = jnp.concatenate([dot(pad_rows, gate_w), dot(pad_rows, up_w)], axis=1)
        pad_terms = pad_terms[:1] + pad_terms[1:2]

        places = jnp.arange(length, dtype=jnp.int32)
        earlier = jnp.sum((boundaries[:, None] < begin + places[None, :]).astype(jnp.int32), axis=0)
        starts = jnp.sum((boundaries[:, None] == begin + places[None, :]).astype(jnp.int32), axis=0)
        slot_ids = jnp.arange(CAP, dtype=jnp.int32)
        picks = (earlier - earlier[0] == slot_ids[:, None]) & (starts > 0)
        q_at = jnp.sum(jnp.where(picks, places[None, :], 0), axis=1)
        sel = picks.astype(BF16)
        span_grad = sum_of_spans(cotangent, earlier + starts - 1)
        rows = encode(byte_states, halo, begin, sel, q_at, enc_gain, w_qkv, w_out)

    gain_rows = main_gain[:width]
    pad_square = jnp.sum(pad_vector * pad_vector)

    def scaled(compact):
        squares = jnp.sum(compact * compact, axis=1, keepdims=True) + pad_square
        scale = lax.rsqrt(squares / main_width + 1e-05)
        return scale, (compact * scale * gain_rows).astype(BF16)

    if not direct:
        gathered = lax.all_gather(rows, PART, axis=0, tiled=True)
        order = jnp.arange(n_span, dtype=jnp.int32).reshape(n_seq, n_member, share)
        order = order.transpose(1, 0, 2).reshape(-1)
        first = block_first(boundaries, jnp.arange(n_dev, dtype=jnp.int32), length)
        compact = dot(place(first, order), gathered)
        scale, main_in = scaled(compact)
        padded = jnp.pad(main_in, ((0, 0), (0, main_width - width)))
        here = lax.dynamic_slice_in_dim(padded, seq * depth, depth, 1)
        gate = dot(here, gate_w) + scale * pad_terms[:, :columns]
        upward = dot(here, up_w) + scale * pad_terms[:, columns:]
        gate, upward = lax.psum((gate, upward), "seq")
        hidden = (jax.nn.silu(gate) * upward).astype(BF16)
        partial = dot_t(hidden, down_t).astype(BF16).reshape(n_member, n_seq * share, depth)
        got = lax.all_to_all(partial, MEMBER, 0, 0, tiled=True)
        summed = jnp.sum(got.astype(F32), axis=0)
        member = lax.axis_index(MEMBER)
        mine = lax.dynamic_slice_in_dim(compact, member * n_seq * share, n_seq * share, 0)
        wide = jnp.concatenate(
            [mine, jnp.broadcast_to(pad_vector, (n_seq * share, main_width - width))], axis=1
        )
        residual = lax.dynamic_slice_in_dim(wide, seq * depth, depth, 1)
        done = (summed + residual).astype(BF16).reshape(n_seq, share, depth)
        spread = lax.all_to_all(done, "seq", 0, 0, tiled=True)
        main_out = spread.transpose(1, 0, 2).reshape(share, main_width)
        return (main_out, span_grad)

    terms = [lax.ppermute(pad_terms, "seq", [(j, 0)]) for j in range(n_seq - 1, 0, -1)]
    terms = kernel_call(terms_kernel, array(2, columns, F32), *terms, name="terms", after=(rows,))
    rows, terms = tie(rows, terms)
    def to_members(value):
        from_chip = swap(value, "mp")
        return value, from_chip, swap(value, "rep"), swap(from_chip, "rep")

    came = [lax.ppermute(rows, "seq", [(j, 0)]) for j in range(1, n_seq)]
    across = lax.ppermute(rows, MEMBER, [(j, 3 - j) for j in range(4)])
    planes = [(rows, swap(rows, "mp"), swap(rows, "rep"), across)]

    def over_cores(values, name):
        quarters = sum(value.shape[0] for value in values) // GROUP // 4
        sent = kernel_call(
            functools.partial(core_step_kernel, len(values)),
            (array(2 * GROUP, depth, BF16),) * quarters,
            *values,
            name=name + "_core",
        )
        return kernel_call(
            functools.partial(chip_step_kernel, len(values)),
            (array(quarters * GROUP, depth, F32), array(quarters * GROUP, depth, BF16)),
            *values,
            *(swap(value, "rep") for value in sent),
            name=name + "_chip",
        )

    hiddens, row_parts, relayed, spread, parts = [], [], [], [], []

    def make_hidden(index, *after):
        low, high = CHUNKS[index]
        halves = [block for plane in planes[max(near_of(low) - 1, 0) : near_of(high - 1) + 1] for block in plane]
        count = (high - low) * share
        hidden, row = kernel_call(
            functools.partial(hidden_at_zero, low, high),
            (array(count, columns, BF16), array(count, width, BF16)),
            where,
            *halves,
            pad_row,
            gain_row,
            gate_w,
            up_w,
            terms,
            name=f"hidden{index}",
            after=after,
        )
        hiddens.append(hidden)
        row_parts.append(row)
        relayed.append(lax.ppermute(hidden, "seq", [(0, 2)]))

    def make_part(index, *after):
        at_one, at_three = spread[index]
        count = row_parts[index].shape[0]
        parts.append(
            kernel_call(
                down_kernel,
                array(count, depth, F32),
                hiddens[index],
                at_one,
                relayed[index],
                at_three,
                down_t,
                row_parts[index],
                pad_row,
                name=f"down{index}",
                after=after,
            )
        )

    def pass_on(index, token):
        relayed[index], token = tie(relayed[index], token)
        spread.append(relay(relayed[index]))
        return relayed[index], token

    value, token = tie(came[0], rows)
    planes.append(to_members(value))
    make_hidden(0, token)
    token = tick("tickz", hiddens[0])
    later = []
    for value in came[1:]:
        value, token = tie(value, token)
        later.append((value, swap(value, "mp"), swap(value, "rep")))
    make_hidden(1, token)
    token = hiddens[1]
    for value, from_chip, from_core in later:
        from_chip, token = tie(from_chip, token)
        planes.append((value, from_chip, from_core, swap(from_chip, "rep")))
    make_hidden(2, token)
    token = hiddens[2]
    for index in range(len(CHUNKS)):
        arrived, token = pass_on(index, token)
        if index == 0:
            make_hidden(3, arrived, token)
            token = hiddens[3]
        token = tick(f"tick{index}", token)
        if index:
            make_part(index - 1, token, arrived)
            token = parts[-1]
        if index == 1:
            sums, to_before, to_after = kernel_call(
                lanes_kernel,
                (array(n_member * share, width, BF16),) + (array(LANE_ROWS, width, BF16),) * 2,
                member_of,
                cotangent,
                name="lanes",
                after=(token,),
            )
            up = [(i, i + 1) for i in range(n_seq - 1)]
            down = [(i + 1, i) for i in range(n_seq - 1)]
            from_both = lax.ppermute(to_after, "seq", up), lax.ppermute(to_before, "seq", down)
            token = sums
    block = kernel_call(
        sums_kernel, array(n_member * share, width, BF16), sums, *from_both, name="span_sums", after=(token,)
    )

    early_own, early_sent = over_cores([*parts[:EARLY], block], "early")
    from_mp = swap(early_sent, "mp")
    make_part(EARLY, early_sent)
    own, sent = over_cores(parts[EARLY:], "late")
    *ready, span_grad = kernel_call(
        add_kernel, (array(GROUP, depth, BF16),) * 4, early_own, from_mp, name="early_add", after=(sent,)
    )

    turned = kernel_call(
        turn_kernel, (array(GROUP, depth, BF16),) * n_seq, own, swap(sent, "mp"), *ready, name="turn"
    )
    arrived = [turned[0]]
    for turn in range(1, n_seq):
        pairs = [(i, (i + turn) % n_seq) for i in range(n_seq)]
        arrived.append(lax.ppermute(turned[turn], "seq", pairs))
    main_out = kernel_call(join_kernel, array(share, main_width, BF16), *arrived, name="join")
    return (main_out, span_grad)


def solution(mesh):
    spread = P(("groups", "seq", "mp", "rep"), None)
    weight = P("seq", ("mp", "rep"))
    placed = (spread, spread, P("groups"), P(), P(), P(), P(), P(), weight, weight, weight)
    return jax.shard_map(
        local, mesh=mesh, in_specs=placed, out_specs=(spread, spread), check_vma=False
    )
```
